256 devices in a mesh: row: 32 (over z, y_lo, core), col: 8 (over y_hi, x).
Axes of the slice: x: 4, y: 4 (y_hi: 2, y_lo: 2; y = y_hi * 2 + y_lo), z: 8, core: 2. Of those that a mesh axis runs over, the one named last changes fastest.
Arguments:
- frames_in: bfloat16 [2, 512, 128, 384], P(None, 'row', 'col'), may hold values from -6 to 6
- grad_out: bfloat16 [2, 512, 128, 384], P(None, 'row', 'col'), may hold values from -6 to 6
- norm_gain: float32 [384], replicated, may hold values from 0.1 to 1.9
- norm_shift: float32 [384], replicated, may hold values from -3 to 3
- qkv_weight: bfloat16 [384, 1152], replicated, may hold values from -0.3125 to 0.3125
- proj_weight: bfloat16 [384, 384], replicated, may hold values from -0.3125 to 0.3125
- bias_table: float32 [675, 12], replicated, may hold values from -6 to 330
- pos_index: int32 [128, 128], replicated, may hold values from 0 to 674
- region_ids: int32 [2, 512, 128], P(None, 'row', 'col'), may hold values from 0 to 3
Outputs:
- block_out: bfloat16 [2, 512, 128, 384], P(None, 'row', 'col')
- grad_input: bfloat16 [2, 512, 128, 384], P(None, 'row', 'col')
- grad_qkv_weight: float32 [384, 1152], replicated
- grad_proj_weight: float32 [384, 384], replicated
- grad_table: float32 [675, 12], replicated
- grad_gain: float32 [384], replicated
- grad_shift: float32 [384], replicated
The draws below stay inside these ranges and needn't reach their ends.
All inputs are finite; a program needn't handle non-finite values.
Results may differ from the reference program's by a relative error of at most 0.0092.
Values may be sent and summed in bfloat16 or wider, within the bound.
No kernel may reach another device: no remote copies, remote signals or barrier semaphores. Data moves between devices by JAX's collectives and lax.ppermute only.
A program may use at most 64 MiB of HBM per device.

```python
import jax
import jax.numpy as jnp
from jax import lax

WIDTH = 384
HEADS = 12
WIN_T = 2
WIN_H = 8
WIN_W = 8
WIN_TOK = 128
TABLE_ROWS = 675
REGIONS = 4
FRAMES = 2
ROWS_DEV = 16
COLS_DEV = 16
ROWS = 512
COLS = 128
TOKENS = 131072


def draw_bias_table(key, part):
    key = jax.random.fold_in(key, 7)
    base_key = jax.random.fold_in(key, 0)
    return jnp.clip(1.5 * jax.random.normal(base_key, (TABLE_ROWS, HEADS), jnp.float32), -6.0, 6.0)


def touch_ends(values, key, least, high):
    place = [jax.random.randint(jax.random.fold_in(key, axis), (), 0, length) for axis, length in enumerate(values.shape)]
    longest = values.shape.index(max(values.shape))
    neighbour = place[:longest] + [(place[longest] + 1) % values.shape[longest]] + place[longest + 1:]
    return values.at[tuple(place)].set(least).at[tuple(neighbour)].set(high)


def shard_levels(stream_key, shape, cuts, smallest, high):
    def one(axis_at, parts):
        draws = jax.random.uniform(jax.random.fold_in(jax.random.fold_in(stream_key, 6), axis_at), (parts,), jnp.float32, smallest / len(cuts), high / len(cuts))
        return jnp.repeat(jnp.exp(draws), shape[axis_at] // parts).reshape((-1,) + (1,) * (len(shape) - axis_at - 1))

    level = one(*cuts[0])
    for cut in cuts[1:]:
        level = level * one(*cut)
    return level


def normal_values(own_key, dims, spread, reach, pieces=(), kind=jnp.bfloat16):
    result = jax.random.normal(own_key, dims, jnp.float32) * spread
    if len(pieces) > 0:
        result = shard_levels(own_key, dims, pieces, -0.22, 0.18) * result
    return jnp.clip(result, min=-reach, max=reach).astype(kind)


def setup_inputs(seed: int = 0) -> dict:
    seeds = jax.random.split(jax.random.key(seed), 10)
    return {
        "frames_in": normal_values(seeds[0], (FRAMES, ROWS, COLS, WIDTH), 1.0, 6.0, ((1, 32), (2, 8))),
        "grad_out": normal_values(seeds[1], (FRAMES, ROWS, COLS, WIDTH), 1.0, 6.0, ((1, 32), (2, 8))),
        "norm_gain": jnp.clip(1.0 + 0.18 * jax.random.normal(seeds[2], (WIDTH,), jnp.float32), 0.1, 1.9),
        "norm_shift": normal_values(seeds[3], (WIDTH,), 0.5, 3.0, (), jnp.float32),
        "qkv_weight": normal_values(seeds[4], (WIDTH, 3 * WIDTH), WIDTH ** -0.5, 0.3125),
        "proj_weight": normal_values(seeds[5], (WIDTH, WIDTH), WIDTH ** -0.5, 0.3125),
        "bias_table": draw_bias_table(jax.random.fold_in(seeds[9], 71), 0),
        "pos_index": touch_ends(jax.random.randint(seeds[7], (WIN_TOK, WIN_TOK), 0, TABLE_ROWS), jax.random.fold_in(seeds[7], 1), 0, TABLE_ROWS - 1).astype(jnp.int32),
        "region_ids": touch_ends(jax.random.randint(seeds[8], (FRAMES, ROWS, COLS), 0, REGIONS), jax.random.fold_in(seeds[8], 1), 0, REGIONS - 1).astype(jnp.int32),
    }


norm_eps = 1e-05

def to_windows(grid_cells):
    frame_count, row_count, col_count = (grid_cells.shape[0], grid_cells.shape[1], grid_cells.shape[2])
    trailing = grid_cells.shape[3:]
    split_up = grid_cells.reshape((frame_count // WIN_T, WIN_T, row_count // WIN_H, WIN_H, col_count // WIN_W, WIN_W) + trailing)
    axis_order = (0, 2, 4, 1, 3, 5) + tuple(range(6, 6 + len(trailing)))
    return split_up.transpose(axis_order).reshape((-1, WIN_TOK) + trailing)

def from_windows(blocks, frame_count, row_count, col_count):
    trailing = blocks.shape[2:]
    split_up = blocks.reshape((frame_count // WIN_T, row_count // WIN_H, col_count // WIN_W, WIN_T, WIN_H, WIN_W) + trailing)
    axis_order = (0, 3, 1, 4, 2, 5) + tuple(range(6, 6 + len(trailing)))
    return split_up.transpose(axis_order).reshape((frame_count, row_count, col_count) + trailing)

def probabilities(queries, key_rows, window_ids, position_bias, score_scale):
    scores = jnp.einsum('wqhd,wkhd->whqk', queries.astype(jnp.float32), key_rows.astype(jnp.float32)) * score_scale + position_bias[None]
    allowed = window_ids[:, None, :, None] == window_ids[:, None, None, :]
    row_max = lax.optimization_barrier(jnp.max(jnp.where(allowed, scores, -1e+30), axis=-1, keepdims=True))
    exp_scores = jnp.exp(jnp.where(allowed, scores - row_max, -1e+30))
    return exp_scores / lax.optimization_barrier(jnp.sum(exp_scores, axis=-1, keepdims=True))

def block_pass(window_x, window_g, window_ids, norm_gain, norm_shift, qkv_weight, proj_weight, position_bias):
    win_count = window_x.shape[0]
    feat_width = window_x.shape[-1]
    head_dim = feat_width // HEADS
    score_scale = head_dim ** (-0.5)
    as_float = window_x.astype(jnp.float32)
    average = lax.optimization_barrier(jnp.mean(as_float, axis=-1, keepdims=True))
    centered = as_float - average
    variance = lax.optimization_barrier(jnp.mean(centered * centered, axis=-1, keepdims=True))
    inv_std = lax.rsqrt(variance + norm_eps)
    x_hat = centered * inv_std
    normed = (x_hat * norm_gain + norm_shift).astype(jnp.bfloat16).reshape(-1, feat_width)
    qkv_all = jnp.dot(normed, qkv_weight, preferred_element_type=jnp.float32).astype(jnp.bfloat16)
    qkv_all = qkv_all.reshape(win_count, WIN_TOK, 3, HEADS, head_dim)
    queries, key_rows, values = (qkv_all[:, :, 0], qkv_all[:, :, 1], qkv_all[:, :, 2])
    attn_prob = probabilities(queries, key_rows, window_ids, position_bias, score_scale)
    prob_bf16 = attn_prob.astype(jnp.bfloat16)
    attended = jnp.einsum('whqk,wkhd->wqhd', prob_bf16.astype(jnp.float32), values.astype(jnp.float32))
    attended = attended.astype(jnp.bfloat16).reshape(-1, feat_width)
    branch = jnp.dot(attended, proj_weight, preferred_element_type=jnp.float32).astype(jnp.bfloat16)
    grad_flat = window_g.reshape(-1, feat_width)
    grad_proj = jnp.dot(attended.T, grad_flat, preferred_element_type=jnp.float32)
    grad_attended = jnp.dot(grad_flat, proj_weight.T, preferred_element_type=jnp.float32).astype(jnp.bfloat16)
    grad_heads = grad_attended.reshape(win_count, WIN_TOK, HEADS, head_dim).astype(jnp.float32)
    grad_prob = jnp.einsum('wqhd,wkhd->whqk', grad_heads, values.astype(jnp.float32))
    row_inner = lax.optimization_barrier(jnp.sum(attn_prob * grad_prob, axis=-1, keepdims=True))
    grad_score = attn_prob * (grad_prob - row_inner)
    table_terms = lax.optimization_barrier(jnp.sum(grad_score, axis=0))
    score_bf16 = (grad_score * score_scale).astype(jnp.bfloat16).astype(jnp.float32)
    grad_query = jnp.einsum('whqk,wkhd->wqhd', score_bf16, key_rows.astype(jnp.float32))
    grad_key = jnp.einsum('whqk,wqhd->wkhd', score_bf16, queries.astype(jnp.float32))
    grad_value = jnp.einsum('whqk,wqhd->wkhd', prob_bf16.astype(jnp.float32), grad_heads)
    grad_qkv = jnp.stack([grad_query, grad_key, grad_value], axis=2).astype(jnp.bfloat16).reshape(-1, 3 * feat_width)
    grad_qkv_w = jnp.dot(normed.T, grad_qkv, preferred_element_type=jnp.float32)
    grad_normed = jnp.dot(grad_qkv, qkv_weight.T, preferred_element_type=jnp.float32)
    flat_hat = x_hat.reshape(-1, feat_width)
    flat_inv = inv_std.reshape(-1, 1)
    grad_gain = lax.optimization_barrier(jnp.sum(grad_normed * flat_hat, axis=0))
    grad_shift = lax.optimization_barrier(jnp.sum(grad_normed, axis=0))
    scaled = grad_normed * norm_gain
    grad_rolled = flat_inv * (scaled - lax.optimization_barrier(jnp.mean(scaled, axis=-1, keepdims=True)) - flat_hat * lax.optimization_barrier(jnp.mean(scaled * flat_hat, axis=-1, keepdims=True)))
    return (branch, grad_rolled.astype(jnp.bfloat16), (grad_proj, grad_qkv_w, table_terms, grad_gain, grad_shift))

def add_pair(left_term, right_term):
    return left_term + right_term

def reference(frames_in, grad_out, norm_gain, norm_shift, qkv_weight, proj_weight, bias_table, pos_index, region_ids):
    half_shift = (-(WIN_T // 2), -(WIN_H // 2), -(WIN_W // 2))
    back_shift = (WIN_T // 2, WIN_H // 2, WIN_W // 2)
    rolled = jnp.roll(frames_in, half_shift, axis=(0, 1, 2))
    grad_branch = jnp.roll(grad_out, half_shift, axis=(0, 1, 2))
    position_bias = jnp.take(bias_table, pos_index, axis=0).transpose(2, 0, 1)
    per_block = FRAMES // WIN_T * (ROWS_DEV // WIN_H) * (COLS_DEV // WIN_W)
    window_x = to_windows(rolled).reshape(-1, per_block, WIN_TOK, WIDTH)
    window_g = to_windows(grad_branch).reshape(-1, per_block, WIN_TOK, WIDTH)
    window_ids = to_windows(region_ids).reshape(-1, per_block, WIN_TOK)

    def one_block(totals, inputs):
        block_x, block_g, block_ids = inputs
        branch, grad_rolled, partials = block_pass(block_x, block_g, block_ids, norm_gain, norm_shift, qkv_weight, proj_weight, position_bias)
        return (jax.tree.map(add_pair, totals, partials), (branch, grad_rolled))
    initial = (jnp.zeros((WIDTH, WIDTH), jnp.float32), jnp.zeros((WIDTH, 3 * WIDTH), jnp.float32), jnp.zeros((HEADS, WIN_TOK, WIN_TOK), jnp.float32), jnp.zeros((WIDTH,), jnp.float32), jnp.zeros((WIDTH,), jnp.float32))
    totals, (branch_all, grad_all) = lax.scan(one_block, initial, (window_x, window_g, window_ids))
    branch_grid = from_windows(branch_all.reshape(-1, WIN_TOK, WIDTH), FRAMES, ROWS, COLS)
    back_grid = from_windows(grad_all.reshape(-1, WIN_TOK, WIDTH), FRAMES, ROWS, COLS)
    block_out = (frames_in.astype(jnp.float32) + jnp.roll(branch_grid, back_shift, axis=(0, 1, 2)).astype(jnp.float32)).astype(jnp.bfloat16)
    grad_input = (grad_out.astype(jnp.float32) + jnp.roll(back_grid, back_shift, axis=(0, 1, 2)).astype(jnp.float32)).astype(jnp.bfloat16)
    norm_factor = TOKENS ** (-0.5)
    grad_table = jax.ops.segment_sum(totals[2].reshape(HEADS, -1).T, pos_index.reshape(-1), num_segments=TABLE_ROWS)
    return (block_out, grad_input, totals[1] * norm_factor, totals[0] * norm_factor, grad_table * norm_factor, totals[3] * norm_factor, totals[4] * norm_factor)
```

```python
import functools

import jax
import jax.numpy as jnp
from jax import lax
from jax.experimental import pallas as pl
from jax.experimental.pallas import tpu as pltpu
from jax.sharding import Mesh
from jax.sharding import PartitionSpec as P

HEADS = 12
WIN_TOK = 128
TABLE_ROWS = 675
WIDTH = 384
HEAD_DIM = 32
GROUP = 128
N_WIN = 4
TOK = N_WIN * WIN_TOK
NORM_EPS = 1e-05
SCALE = HEAD_DIM**-0.5

ROW_PROJ = 9 * WIDTH
ROW_TABLE = 12 * WIDTH
ROW_NORM = ROW_TABLE + 96
PACK_ROWS = 4864

F32 = jnp.float32
BF16 = jnp.bfloat16
VMEM_LIMIT = 50 * 1024 * 1024

NN = (((1,), (0,)), ((), ()))
NT = (((1,), (1,)), ((), ()))
TN = (((0,), (0,)), ((), ()))


def mm(a, b, dims):
    return lax.dot_general(a, b, dims, preferred_element_type=F32)


def whole(n):
    return [pl.BlockSpec(memory_space=pltpu.VMEM)] * n


def bias_kernel(pos_ref, table_ref, bias_ref):
    def rows(step, carry):
        at = pl.multiple_of(step * 8, 8)
        idx = pos_ref[pl.ds(at, 8), :]
        low = idx & 127
        high = idx >> 7
        for h in range(HEADS):
            got = None
            for k in range(6):
                chunk = jnp.broadcast_to(table_ref[h : h + 1, k * 128 : (k + 1) * 128], (8, 128))
                part = jnp.take_along_axis(chunk, low, axis=1)
                got = part if k == 0 else jnp.where(high == k, part, got)
            bias_ref[h, pl.ds(at, 8), :] = got
        return carry

    lax.fori_loop(0, 16, rows, 0)


def gather_bias(pos_t, table_t):
    return pl.pallas_call(
        bias_kernel,
        out_shape=jax.ShapeDtypeStruct((HEADS, WIN_TOK, WIN_TOK), F32),
        in_specs=whole(2),
        out_specs=pl.BlockSpec(memory_space=pltpu.VMEM),
        cost_estimate=pl.CostEstimate(flops=4_000_000, bytes_accessed=900_000, transcendentals=0),
        name="gather_bias",
    )(pos_t, table_t)


def window_tokens(ref, wr, wc):
    block = ref[:, 8 * wr : 8 * wr + 8, :, :].astype(F32)
    return block[:, :, 8 * wc : 8 * wc + 8, :].reshape(WIN_TOK, WIDTH)


def store_tile(ref, tokens):
    for wr in range(2):
        pair = [
            tokens[(2 * wr + wc) * WIN_TOK : (2 * wr + wc + 1) * WIN_TOK].reshape(2, 8, 8, WIDTH)
            for wc in range(2)
        ]
        ref[:, 8 * wr : 8 * wr + 8, :, :] = jnp.concatenate(pair, axis=2).astype(BF16)


def main_kernel(
    x_ref, g_ref, gain_ref, shift_ref, wqkv_ref, wproj_ref, bias_ref, id_row_ref, id_col_ref,
    pos_ref, branch_ref, back_ref, pack_ref,
    hat_s, inv_s, normed_s, g_s, qkv_s, da_s, att_s, gqkv_s, table_s,
):
    for wr in range(2):
        for wc in range(2):
            at = (2 * wr + wc) * WIN_TOK
            rows = slice(at, at + WIN_TOK)
            x = window_tokens(x_ref, wr, wc)
            centered = x - jnp.mean(x, axis=-1, keepdims=True)
            variance = jnp.mean(centered * centered, axis=-1, keepdims=True)
            inv_std = lax.rsqrt(variance + NORM_EPS)
            x_hat = centered * inv_std
            hat_s[rows, :] = x_hat
            inv_s[rows, :] = jnp.broadcast_to(inv_std, (WIN_TOK, 128))
            normed_s[rows, :] = (x_hat * gain_ref[...] + shift_ref[...]).astype(BF16)
            g_s[rows, :] = window_tokens(g_ref, wr, wc).astype(BF16)
    for p in range(3):
        part = mm(normed_s[...], wqkv_ref[:, p * WIDTH : (p + 1) * WIDTH], NN).astype(BF16)
        for k in range(3):
            qkv_s[3 * p + k] = part[:, k * GROUP : (k + 1) * GROUP]
    part = mm(g_s[...], wproj_ref[...], NT).astype(BF16)
    for k in range(3):
        da_s[k] = part[:, k * GROUP : (k + 1) * GROUP]

    table_s[...] = jnp.zeros_like(table_s)
    lane = lax.broadcasted_iota(jnp.int32, (WIN_TOK, GROUP), 1) // HEAD_DIM

    def attend(step, carry):
        w = step // 3
        k = step % 3
        rows = pl.ds(pl.multiple_of(w * WIN_TOK, WIN_TOK), WIN_TOK)
        q = qkv_s[k, rows, :]
        key = qkv_s[3 + k, rows, :]
        v = qkv_s[6 + k, rows, :]
        da = da_s[k, rows, :]
        shut = jnp.where(id_col_ref[w] == id_row_ref[w], 0.0, -1e30)
        zero = jnp.zeros_like(q)
        heads = []
        for h in range(4):
            mine = lane == h
            heads.append(tuple(jnp.where(mine, a, zero) for a in (q, key, v, da)))
        probs, grads = [], []
        for h in range(4):
            _, key_h, v_h, _ = heads[h]
            score = mm(key_h, q, NT) * SCALE + bias_ref[4 * k + h] + shut
            top = jnp.max(score, axis=0, keepdims=True)
            e = jnp.exp(score - top)
            prob = e * (1.0 / jnp.sum(e, axis=0, keepdims=True))
            grad_prob = mm(v_h, da, NT)
            inner = jnp.sum(prob * grad_prob, axis=0, keepdims=True)
            grad_score = prob * (grad_prob - inner)
            table_s[4 * k + h] += grad_score
            probs.append(prob.astype(BF16))
            grads.append((grad_score * SCALE).astype(BF16))
        prob_rows = jnp.concatenate(probs, axis=0)
        grad_rows = jnp.concatenate(grads, axis=0)
        q_all, key_all, v_all, da_all = (
            jnp.concatenate([heads[h][n] for h in range(4)], axis=0) for n in range(4)
        )
        att_s[k, rows, :] = mm(prob_rows, v_all, TN).astype(BF16)
        gqkv_s[k, rows, :] = mm(grad_rows, key_all, TN).astype(BF16)
        gqkv_s[3 + k, rows, :] = mm(jnp.concatenate(grads, axis=1), q_all, NN).astype(BF16)
        gqkv_s[6 + k, rows, :] = mm(jnp.concatenate(probs, axis=1), da_all, NN).astype(BF16)
        return carry

    lax.fori_loop(0, 12, attend, 0)

    attended = jnp.concatenate([att_s[k] for k in range(3)], axis=1)
    store_tile(branch_ref, mm(attended, wproj_ref[...], NN))
    grad_proj = mm(attended, g_s[...], TN)
    for k in range(3):
        at = ROW_PROJ + k * WIDTH
        pack_ref[at : at + WIDTH, :] = grad_proj[:, k * GROUP : (k + 1) * GROUP].astype(BF16)

    grad_normed = None
    for p in range(3):
        grad_part = jnp.concatenate([gqkv_s[3 * p + k] for k in range(3)], axis=1)
        grad_w = mm(normed_s[...], grad_part, TN)
        for k in range(3):
            at = (3 * p + k) * WIDTH
            pack_ref[at : at + WIDTH, :] = grad_w[:, k * GROUP : (k + 1) * GROUP].astype(BF16)
        term = mm(grad_part, wqkv_ref[:, p * WIDTH : (p + 1) * WIDTH], NT)
        grad_normed = term if p == 0 else grad_normed + term
    x_hat = hat_s[...]
    grad_gain = jnp.sum(grad_normed * x_hat, axis=0, keepdims=True)
    grad_shift = jnp.sum(grad_normed, axis=0, keepdims=True)
    scaled = grad_normed * gain_ref[...]
    grad_rolled = inv_s[:, 0:1] * (
        scaled
        - jnp.mean(scaled, axis=-1, keepdims=True)
        - x_hat * jnp.mean(scaled * x_hat, axis=-1, keepdims=True)
    )
    store_tile(back_ref, grad_rolled)

    low_bins = lax.broadcasted_iota(jnp.int32, (256, WIN_TOK), 0)

    def bins(step, acc):
        left, right = [], []
        for n in range(2):
            j = 2 * step + n
            idx = pos_ref[pl.ds(j, 1), :]
            high = idx >> 8
            terms = table_s[:, j, :]
            left.append(
                jnp.concatenate([jnp.where(high == a, terms, 0.0) for a in range(3)], axis=0)
            )
            right.append(jnp.where(low_bins == (idx & 255), 1.0, 0.0).astype(BF16))
        return acc + mm(
            jnp.concatenate(left, axis=1).astype(BF16), jnp.concatenate(right, axis=1), NT
        )

    table = lax.fori_loop(0, WIN_TOK // 2, bins, jnp.zeros((48, 256), F32))
    for n in range(2):
        at = ROW_TABLE + 48 * n
        pack_ref[at : at + 48, :] = table[:, 128 * n : 128 * (n + 1)].astype(BF16)
    norm_rows = [a[:, k * 128 : (k + 1) * 128] for a in (grad_gain, grad_shift) for k in range(3)]
    norm_rows.append(jnp.zeros((10, 128), F32))
    pack_ref[ROW_NORM : ROW_NORM + 16, :] = jnp.concatenate(norm_rows, axis=0).astype(BF16)
    pack_ref[ROW_NORM + 16 :, :] = jnp.zeros((PACK_ROWS - ROW_NORM - 16, 128), BF16)


def main_call(*args):
    tile = jax.ShapeDtypeStruct((2, 16, 16, WIDTH), BF16)
    return pl.pallas_call(
        main_kernel,
        out_shape=(tile, tile, jax.ShapeDtypeStruct((PACK_ROWS, 128), BF16)),
        in_specs=whole(len(args)),
        out_specs=tuple(whole(3)),
        scratch_shapes=[
            pltpu.VMEM((TOK, WIDTH), F32),
            pltpu.VMEM((TOK, 128), F32),
            pltpu.VMEM((TOK, WIDTH), BF16),
            pltpu.VMEM((TOK, WIDTH), BF16),
            pltpu.VMEM((9, TOK, GROUP), BF16),
            pltpu.VMEM((3, TOK, GROUP), BF16),
            pltpu.VMEM((3, TOK, GROUP), BF16),
            pltpu.VMEM((9, TOK, GROUP), BF16),
            pltpu.VMEM((16, WIN_TOK, WIN_TOK), F32),
        ],
        compiler_params=pltpu.CompilerParams(vmem_limit_bytes=VMEM_LIMIT),
        cost_estimate=pl.CostEstimate(
            flops=4_000_000_000, bytes_accessed=6_000_000, transcendentals=800_000
        ),
        name="block_pass",
    )(*args)


def unpack_kernel(factor, pack_ref, qkv_ref, proj_ref, table_ref, norm_ref):
    for k in range(12):
        block = pack_ref[k * WIDTH : (k + 1) * WIDTH, :].astype(F32) * factor
        if k < 9:
            qkv_ref[:, k * 128 : (k + 1) * 128] = block
        else:
            proj_ref[:, (k - 9) * 128 : (k - 8) * 128] = block
    table = pack_ref[ROW_TABLE : ROW_TABLE + 96, :].astype(F32) * factor
    for a in range(3):
        for n in range(2):
            table_ref[:, (2 * a + n) * 128 : (2 * a + n + 1) * 128] = table[
                48 * n + 16 * a : 48 * n + 16 * a + 16
            ]
    norm_ref[...] = pack_ref[ROW_NORM : ROW_NORM + 16, :].astype(F32) * factor


def unpack(pack, factor):
    return pl.pallas_call(
        functools.partial(unpack_kernel, factor),
        out_shape=(
            jax.ShapeDtypeStruct((WIDTH, 3 * WIDTH), F32),
            jax.ShapeDtypeStruct((WIDTH, WIDTH), F32),
            jax.ShapeDtypeStruct((16, 768), F32),
            jax.ShapeDtypeStruct((16, 128), F32),
        ),
        in_specs=whole(1),
        out_specs=tuple(whole(4)),
        compiler_params=pltpu.CompilerParams(vmem_limit_bytes=VMEM_LIMIT),
        cost_estimate=pl.CostEstimate(flops=600_000, bytes_accessed=3_600_000, transcendentals=0),
        name="unpack_sums",
    )(pack)


ROW = ("z", "l", "c")
COL = ("h", "x")
ALL = ROW + COL


def shifted(value, row_step, col_step):
    rows = lax.axis_size(ROW)
    cols = lax.axis_size(COL)
    pairs = [
        (r * cols + c, ((r + row_step) % rows) * cols + (c + col_step) % cols)
        for r in range(rows)
        for c in range(cols)
    ]
    return lax.ppermute(value, ALL, pairs)


def sum_scatter(pack, axes):
    count = lax.axis_size(axes)
    got = lax.all_to_all(pack.reshape(count, -1, 128), axes, 0, 0)
    return jnp.sum(got.astype(F32), axis=0).astype(BF16)


def spread(part, axes):
    count = lax.axis_size(axes)
    sent = jnp.broadcast_to(part[None], (count,) + part.shape)
    return lax.all_to_all(sent, axes, 0, 0)


def sum_everywhere(pack):
    part = sum_scatter(pack, ("c",))
    part = sum_scatter(part, ("l", "h", "x"))
    part = jnp.sum(spread(part, ("z",)).astype(F32), axis=0).astype(BF16)
    part = spread(part, ("l", "h", "x")).reshape(-1, 128)
    return spread(part, ("c",)).reshape(PACK_ROWS, 128)


def body(
    frames_in, grad_out, norm_gain, norm_shift, qkv_weight, proj_weight, bias_table, pos_index,
    region_ids,
):
    frame_count, row_count, col_count, _ = frames_in.shape
    token_total = frame_count * row_count * col_count * lax.axis_size(ALL)
    both = (frames_in, grad_out)
    below = shifted(jnp.stack([a[:, :4] for a in both]), -1, 0)
    right = shifted(jnp.stack([a[:, :, :4] for a in both]), 0, -1)
    corner = shifted(jnp.stack([a[:, :4, :4] for a in both]), -1, -1)
    rolled = []
    for n, a in enumerate(both):
        upper = jnp.concatenate([a[:, 4:, 4:], right[n][:, 4:]], axis=2)
        lower = jnp.concatenate([below[n][:, :, 4:], corner[n]], axis=2)
        tile = jnp.concatenate([upper, lower], axis=1)
        rolled.append(jnp.concatenate([tile[1:], tile[:1]], axis=0))

    pos_t = pos_index.T
    table_t = jnp.pad(bias_table.T, ((0, 4), (0, 768 - TABLE_ROWS)))
    bias = gather_bias(pos_t, table_t)
    ids = region_ids.reshape(2, 2, 8, 2, 8).transpose(1, 3, 0, 2, 4).reshape(N_WIN, WIN_TOK)
    branch, back, pack = main_call(
        rolled[0], rolled[1], norm_gain[None], norm_shift[None], qkv_weight, proj_weight, bias,
        ids[:, None, :], ids[:, :, None], pos_t,
    )
    flipped = [jnp.concatenate([a[1:], a[:1]], axis=0) for a in (branch, back)]
    above = shifted(jnp.stack([a[:, 12:, :12] for a in flipped]), 1, 0)
    left = shifted(jnp.stack([a[:, :12, 12:] for a in flipped]), 0, 1)
    angle = shifted(jnp.stack([a[:, 12:, 12:] for a in flipped]), 1, 1)
    outs = []
    for n, a in enumerate(both):
        upper = jnp.concatenate([angle[n], above[n]], axis=2)
        lower = jnp.concatenate([left[n], flipped[n][:, :12, :12]], axis=2)
        moved = jnp.concatenate([upper, lower], axis=1)
        outs.append((a.astype(F32) + moved.astype(F32)).astype(BF16))

    total = sum_everywhere(pack)
    grad_qkv, grad_proj, table, norm = unpack(total, token_total**-0.5)
    grad_table = table[:HEADS, :TABLE_ROWS].T
    grad_gain = norm[0:3].reshape(WIDTH)
    grad_shift = norm[3:6].reshape(WIDTH)
    return outs[0], outs[1], grad_qkv, grad_proj, grad_table, grad_gain, grad_shift


def solution(mesh):
    rows, cols = mesh.devices.shape
    fine = Mesh(mesh.devices.reshape(rows // 4, 2, 2, 2, cols // 2), ALL)
    tile = P(None, ROW, COL, None)
    return jax.shard_map(
        body,
        mesh=fine,
        in_specs=(tile, tile, P(), P(), P(), P(), P(), P(), P(None, ROW, COL)),
        out_specs=(tile, tile, P(), P(), P(), P(), P()),
        check_vma=False,
    )
```

```python
import functools

import jax
import jax.numpy as jnp
from jax import lax
from jax.experimental import pallas as pl
from jax.experimental.pallas import tpu as pltpu
from jax.sharding import Mesh
from jax.sharding import PartitionSpec as P

HEADS = 12
WIN_TOK = 128
TABLE_ROWS = 675
WIDTH = 384
HEAD_DIM = 32
GROUP = 128
N_WIN = 4
TOK = N_WIN * WIN_TOK
NORM_EPS = 1e-05
SCALE = HEAD_DIM**-0.5

ROW_PROJ = 9 * WIDTH
ROW_TABLE = 12 * WIDTH
ROW_NORM = ROW_TABLE + 96
PACK_ROWS = 4864
HALF = PACK_ROWS // 2

F32 = jnp.float32
BF16 = jnp.bfloat16
VMEM_LIMIT = 20 * 1024 * 1024

NN = (((1,), (0,)), ((), ()))
NT = (((1,), (1,)), ((), ()))
TN = (((0,), (0,)), ((), ()))


def mm(a, b, dims):
    return lax.dot_general(a, b, dims, preferred_element_type=F32)


def whole(n):
    return [pl.BlockSpec(memory_space=pltpu.VMEM)] * n


def in_vmem(shape, dtype):
    return pltpu.VMEM(shape, dtype)


def edge_kernel(x_ref, g_ref, below_ref, right_ref, corner_ref, x_s, g_s, sems):
    copies = [
        pltpu.make_async_copy(x_ref, x_s, sems.at[0]),
        pltpu.make_async_copy(g_ref, g_s, sems.at[1]),
    ]
    for copy in copies:
        copy.start()
    for n, ref in enumerate((x_s, g_s)):
        copies[n].wait()
        below_ref[n] = ref[:, 0:4, :, :]
        right_ref[n] = ref[:, 4:16, 0:4, :]
        corner_ref[n] = ref[:, 0:4, 0:4, :]


def edges(x, g):
    return pl.pallas_call(
        edge_kernel,
        out_shape=(
            in_vmem((2, 2, 4, 16, WIDTH), BF16),
            in_vmem((2, 2, 12, 4, WIDTH), BF16),
            in_vmem((2, 2, 4, 4, WIDTH), BF16),
        ),
        in_specs=[pl.BlockSpec(memory_space=pltpu.HBM)] * 2,
        out_specs=tuple(whole(3)),
        scratch_shapes=[
            pltpu.VMEM((2, 16, 16, WIDTH), BF16),
            pltpu.VMEM((2, 16, 16, WIDTH), BF16),
            pltpu.SemaphoreType.DMA((2,)),
        ],
        compiler_params=pltpu.CompilerParams(vmem_limit_bytes=VMEM_LIMIT),
        cost_estimate=pl.CostEstimate(flops=0, bytes_accessed=1_200_000, transcendentals=0),
        name="edges",
    )(*(pltpu.with_memory_space_constraint(a, pltpu.HBM) for a in (x, g)))


def bias_kernel(pos_ref, table_ref, bias_ref, pos_t_ref, table_s):
    pos_t_ref[...] = pos_ref[...].T
    table_s[...] = jnp.zeros_like(table_s)
    table_s[0:HEADS, 0:TABLE_ROWS] = table_ref[...]

    def rows(step, carry):
        at = pl.multiple_of(step * 8, 8)
        idx = pos_t_ref[pl.ds(at, 8), :]
        low = idx & 127
        high = idx >> 7
        for h in range(HEADS):
            got = None
            for k in range(6):
                chunk = jnp.broadcast_to(table_s[h : h + 1, k * 128 : (k + 1) * 128], (8, 128))
                part = jnp.take_along_axis(chunk, low, axis=1)
                got = part if k == 0 else jnp.where(high == k, part, got)
            bias_ref[h, pl.ds(at, 8), :] = got
        return carry

    lax.fori_loop(0, 16, rows, 0)


def gather_bias(pos_index, table_t):
    return pl.pallas_call(
        bias_kernel,
        out_shape=(
            in_vmem((HEADS, WIN_TOK, WIN_TOK), F32),
            in_vmem((WIN_TOK, WIN_TOK), jnp.int32),
        ),
        in_specs=whole(2),
        out_specs=tuple(whole(2)),
        scratch_shapes=[pltpu.VMEM((16, 768), F32)],
        compiler_params=pltpu.CompilerParams(vmem_limit_bytes=VMEM_LIMIT),
        cost_estimate=pl.CostEstimate(flops=4_000_000, bytes_accessed=900_000, transcendentals=0),
        name="gather_bias",
    )(pos_index, table_t)


def window_tokens(ref, wr, wc):
    block = ref[:, 8 * wr : 8 * wr + 8, :, :].astype(F32)
    return block[:, :, 8 * wc : 8 * wc + 8, :].reshape(WIN_TOK, WIDTH)


def store_tile(ref, tokens):
    for wr in range(2):
        pair = [
            tokens[(2 * wr + wc) * WIN_TOK : (2 * wr + wc + 1) * WIN_TOK].reshape(2, 8, 8, WIDTH)
            for wc in range(2)
        ]
        ref[:, 8 * wr : 8 * wr + 8, :, :] = jnp.concatenate(pair, axis=2).astype(BF16)


def main_kernel(
    x_ref, g_ref, gain_ref, shift_ref, wqkv_ref, wproj_ref, bias_ref, id_ref,
    pos_ref, me_ref, kept_ref, sent_ref, att_s, hat_s, inv_s, gnorm_ref,
    normed_s, g_s, qkv_s, da_s, gqkv_s, table_s, shut_s, pack_ref,
):
    for wr in range(2):
        for wc in range(2):
            at = (2 * wr + wc) * WIN_TOK
            rows = slice(at, at + WIN_TOK)
            x = window_tokens(x_ref, wr, wc)
            centered = x - jnp.mean(x, axis=-1, keepdims=True)
            variance = jnp.mean(centered * centered, axis=-1, keepdims=True)
            inv_std = lax.rsqrt(variance + NORM_EPS)
            x_hat = centered * inv_std
            hat_s[rows, :] = x_hat
            inv_s[rows, :] = jnp.broadcast_to(inv_std, (WIN_TOK, 128))
            normed_s[rows, :] = (x_hat * gain_ref[...] + shift_ref[...]).astype(BF16)
            g_s[rows, :] = window_tokens(g_ref, wr, wc).astype(BF16)
    for p in range(3):
        part = mm(normed_s[...], wqkv_ref[:, p * WIDTH : (p + 1) * WIDTH], NN).astype(BF16)
        for k in range(3):
            qkv_s[3 * p + k] = part[:, k * GROUP : (k + 1) * GROUP]
    part = mm(g_s[...], wproj_ref[...], NT).astype(BF16)
    for k in range(3):
        da_s[k] = part[:, k * GROUP : (k + 1) * GROUP]

    for w in range(N_WIN):
        ids = jnp.broadcast_to(id_ref[w : w + 1, :], (WIN_TOK, WIN_TOK))
        shut_s[w] = jnp.where(ids.T == ids, 0.0, -1e30)
    table_s[...] = jnp.zeros_like(table_s)
    lane = lax.broadcasted_iota(jnp.int32, (WIN_TOK, GROUP), 1) // HEAD_DIM

    def attend(step, carry):
        w = step // 3
        k = step % 3
        rows = pl.ds(pl.multiple_of(w * WIN_TOK, WIN_TOK), WIN_TOK)
        q = qkv_s[k, rows, :]
        key = qkv_s[3 + k, rows, :]
        v = qkv_s[6 + k, rows, :]
        da = da_s[k, rows, :]
        shut = shut_s[w]
        zero = jnp.zeros_like(q)
        heads = []
        for h in range(4):
            mine = lane == h
            heads.append(tuple(jnp.where(mine, a, zero) for a in (q, key, v, da)))
        probs, grads = [], []
        for h in range(4):
            _, key_h, v_h, _ = heads[h]
            score = mm(key_h, q, NT) * SCALE + bias_ref[4 * k + h] + shut
            top = jnp.max(score, axis=0, keepdims=True)
            e = jnp.exp(score - top)
            prob = e * (1.0 / jnp.sum(e, axis=0, keepdims=True))
            grad_prob = mm(v_h, da, NT)
            inner = jnp.sum(prob * grad_prob, axis=0, keepdims=True)
            grad_score = prob * (grad_prob - inner)
            table_s[4 * k + h] += grad_score
            probs.append(prob.astype(BF16))
            grads.append((grad_score * SCALE).astype(BF16))
        prob_rows = jnp.concatenate(probs, axis=0)
        grad_rows = jnp.concatenate(grads, axis=0)
        q_all, key_all, v_all, da_all = (
            jnp.concatenate([heads[h][n] for h in range(4)], axis=0) for n in range(4)
        )
        att_s[k, rows, :] = mm(prob_rows, v_all, TN).astype(BF16)
        gqkv_s[k, rows, :] = mm(grad_rows, key_all, TN).astype(BF16)
        gqkv_s[3 + k, rows, :] = mm(jnp.concatenate(grads, axis=1), q_all, NN).astype(BF16)
        gqkv_s[6 + k, rows, :] = mm(jnp.concatenate(probs, axis=1), da_all, NN).astype(BF16)
        return carry

    lax.fori_loop(0, 12, attend, 0)

    attended = jnp.concatenate([att_s[k] for k in range(3)], axis=1)
    grad_proj = mm(attended, g_s[...], TN)
    for k in range(3):
        at = ROW_PROJ + k * WIDTH
        pack_ref[at : at + WIDTH, :] = grad_proj[:, k * GROUP : (k + 1) * GROUP].astype(BF16)

    grad_normed = None
    for p in range(3):
        grad_part = jnp.concatenate([gqkv_s[3 * p + k] for k in range(3)], axis=1)
        grad_w = mm(normed_s[...], grad_part, TN)
        for k in range(3):
            at = (3 * p + k) * WIDTH
            pack_ref[at : at + WIDTH, :] = grad_w[:, k * GROUP : (k + 1) * GROUP].astype(BF16)
        term = mm(grad_part, wqkv_ref[:, p * WIDTH : (p + 1) * WIDTH], NT)
        grad_normed = term if p == 0 else grad_normed + term
    x_hat = hat_s[...]
    grad_gain = jnp.sum(grad_normed * x_hat, axis=0, keepdims=True)
    grad_shift = jnp.sum(grad_normed, axis=0, keepdims=True)
    gnorm_ref[...] = grad_normed

    low_bins = lax.broadcasted_iota(jnp.int32, (128, WIN_TOK), 0)

    def bins(step, acc):
        at = pl.multiple_of(step * 8, 8)
        index = pos_ref[pl.ds(at, 8), :]
        block = jnp.swapaxes(table_s[:, pl.ds(at, 8), :], 0, 1)
        for n in range(0, 8, 2):
            left, right = [], []
            for j in (n, n + 1):
                idx = index[j : j + 1]
                high = idx >> 7
                terms = block[j]
                left.append(
                    jnp.concatenate([jnp.where(high == a, terms, 0.0) for a in range(6)], axis=0)
                )
                right.append(jnp.where(low_bins == (idx & 127), 1.0, 0.0))
            acc = acc + mm(
                jnp.concatenate(left, axis=1).astype(BF16),
                jnp.concatenate(right, axis=1).astype(BF16),
                NT,
            )
        return acc

    table = lax.fori_loop(0, WIN_TOK // 8, bins, jnp.zeros((96, 128), F32))
    pack_ref[ROW_TABLE : ROW_TABLE + 96, :] = table.astype(BF16)
    norm_rows = [a[:, k * 128 : (k + 1) * 128] for a in (grad_gain, grad_shift) for k in range(3)]
    norm_rows.append(jnp.zeros((10, 128), F32))
    pack_ref[ROW_NORM : ROW_NORM + 16, :] = jnp.concatenate(norm_rows, axis=0).astype(BF16)
    pack_ref[ROW_NORM + 16 :, :] = jnp.zeros((PACK_ROWS - ROW_NORM - 16, 128), BF16)
    me = me_ref[0]
    kept_ref[...] = pack_ref[pl.ds(pl.multiple_of(me * HALF, HALF), HALF), :]
    sent_ref[...] = pack_ref[pl.ds(pl.multiple_of((1 - me) * HALF, HALF), HALF), :]


def main_call(*args):
    return pl.pallas_call(
        main_kernel,
        out_shape=(
            in_vmem((HALF, 128), BF16),
            in_vmem((HALF, 128), BF16),
            in_vmem((3, TOK, GROUP), BF16),
            in_vmem((TOK, WIDTH), F32),
            in_vmem((TOK, 128), F32),
            in_vmem((TOK, WIDTH), F32),
        ),
        in_specs=whole(len(args) - 1) + [pl.BlockSpec(memory_space=pltpu.SMEM)],
        out_specs=tuple(whole(6)),
        scratch_shapes=[
            pltpu.VMEM((TOK, WIDTH), BF16),
            pltpu.VMEM((TOK, WIDTH), BF16),
            pltpu.VMEM((9, TOK, GROUP), BF16),
            pltpu.VMEM((3, TOK, GROUP), BF16),
            pltpu.VMEM((9, TOK, GROUP), BF16),
            pltpu.VMEM((16, WIN_TOK, WIN_TOK), F32),
            pltpu.VMEM((N_WIN, WIN_TOK, WIN_TOK), F32),
            pltpu.VMEM((PACK_ROWS, 128), BF16),
        ],
        compiler_params=pltpu.CompilerParams(vmem_limit_bytes=VMEM_LIMIT),
        cost_estimate=pl.CostEstimate(
            flops=4_000_000_000, bytes_accessed=6_000_000, transcendentals=800_000
        ),
        name="block_pass",
    )(*args)


def token_kernel(att_ref, hat_ref, inv_ref, gnorm_ref, gain_ref, wproj_ref, branch_ref, back_ref):
    attended = jnp.concatenate([att_ref[k] for k in range(3)], axis=1)
    store_tile(branch_ref, mm(attended, wproj_ref[...], NN))
    x_hat = hat_ref[...]
    scaled = gnorm_ref[...] * gain_ref[...]
    store_tile(
        back_ref,
        inv_ref[:, 0:1]
        * (
            scaled
            - jnp.mean(scaled, axis=-1, keepdims=True)
            - x_hat * jnp.mean(scaled * x_hat, axis=-1, keepdims=True)
        ),
    )


def token_call(*args):
    tile = in_vmem((2, 16, 16, WIDTH), BF16)
    return pl.pallas_call(
        token_kernel,
        out_shape=(tile, tile),
        in_specs=whole(len(args)),
        out_specs=tuple(whole(2)),
        compiler_params=pltpu.CompilerParams(vmem_limit_bytes=VMEM_LIMIT),
        cost_estimate=pl.CostEstimate(
            flops=200_000_000, bytes_accessed=4_000_000, transcendentals=0
        ),
        name="token_pass",
    )(*args)


def unpack_kernel(
    factor, me_ref, own_ref, other_ref, qkv_ref, proj_ref, table_ref, gain_ref, shift_ref, pack_ref
):
    me = me_ref[0]
    pack_ref[pl.ds(pl.multiple_of(me * HALF, HALF), HALF), :] = own_ref[...]
    pack_ref[pl.ds(pl.multiple_of((1 - me) * HALF, HALF), HALF), :] = other_ref[...]
    for k in range(12):
        block = pack_ref[k * WIDTH : (k + 1) * WIDTH, :].astype(F32) * factor
        if k < 9:
            qkv_ref[:, k * 128 : (k + 1) * 128] = block
        else:
            proj_ref[:, (k - 9) * 128 : (k - 8) * 128] = block
    table = pack_ref[ROW_TABLE : ROW_TABLE + 96, :].astype(F32) * factor
    wide = jnp.concatenate([table[16 * a : 16 * a + 16] for a in range(6)], axis=1)
    table_ref[...] = wide[0:HEADS, 0:TABLE_ROWS]
    norm = pack_ref[ROW_NORM : ROW_NORM + 16, :].astype(F32) * factor
    for n, ref in enumerate((gain_ref, shift_ref)):
        for k in range(3):
            ref[:, k * 128 : (k + 1) * 128] = norm[3 * n + k : 3 * n + k + 1]


def unpack(me, own, other, factor):
    return pl.pallas_call(
        functools.partial(unpack_kernel, factor),
        out_shape=(
            jax.ShapeDtypeStruct((WIDTH, 3 * WIDTH), F32),
            jax.ShapeDtypeStruct((WIDTH, WIDTH), F32),
            jax.ShapeDtypeStruct((HEADS, TABLE_ROWS), F32),
            jax.ShapeDtypeStruct((1, WIDTH), F32),
            jax.ShapeDtypeStruct((1, WIDTH), F32),
        ),
        in_specs=[pl.BlockSpec(memory_space=pltpu.SMEM)] + whole(2),
        out_specs=tuple(whole(5)),
        scratch_shapes=[pltpu.VMEM((PACK_ROWS, 128), BF16)],
        compiler_params=pltpu.CompilerParams(vmem_limit_bytes=VMEM_LIMIT),
        cost_estimate=pl.CostEstimate(flops=600_000, bytes_accessed=3_600_000, transcendentals=0),
        name="unpack_sums",
    )(me, own, other)


def add_kernel(a_ref, b_ref, out_ref):
    out_ref[...] = (a_ref[...].astype(F32) + b_ref[...].astype(F32)).astype(BF16)


def add_halves(a, b):
    return pl.pallas_call(
        add_kernel,
        out_shape=in_vmem((HALF, 128), BF16),
        in_specs=whole(2),
        out_specs=pl.BlockSpec(memory_space=pltpu.VMEM),
        compiler_params=pltpu.CompilerParams(vmem_limit_bytes=VMEM_LIMIT),
        cost_estimate=pl.CostEstimate(flops=300_000, bytes_accessed=1_800_000, transcendentals=0),
        name="add_halves",
    )(a, b)


def copies_kernel(parts_ref, out_ref):
    total = parts_ref[0].astype(F32)
    for n in range(1, parts_ref.shape[0]):
        total += parts_ref[n].astype(F32)
    total = total.astype(BF16)
    for n in range(out_ref.shape[0]):
        out_ref[n] = total


def sum_copies(parts, count):
    return pl.pallas_call(
        copies_kernel,
        out_shape=in_vmem((count,) + parts.shape[1:], BF16),
        in_specs=whole(1),
        out_specs=pl.BlockSpec(memory_space=pltpu.VMEM),
        compiler_params=pltpu.CompilerParams(vmem_limit_bytes=VMEM_LIMIT),
        cost_estimate=pl.CostEstimate(flops=300_000, bytes_accessed=1_200_000, transcendentals=0),
        name="sum_copies",
    )(parts)


ROW = ("z", "l", "c")
COL = ("h", "x")
ALL = ROW + COL


def shifted(value, row_step, col_step):
    rows = lax.axis_size(ROW)
    cols = lax.axis_size(COL)
    pairs = [
        (r * cols + c, ((r + row_step) % rows) * cols + (c + col_step) % cols)
        for r in range(rows)
        for c in range(cols)
    ]
    return lax.ppermute(value, ALL, pairs)


def exchange(parts, axes):
    return lax.all_to_all(parts, axes, 0, 0)


def swap_cores(value):
    count = lax.axis_size(ALL)
    cols = lax.axis_size(COL)
    return lax.ppermute(value, ALL, [(i, i ^ cols) for i in range(count)])


def body(
    frames_in, grad_out, norm_gain, norm_shift, qkv_weight, proj_weight, bias_table, pos_index,
    region_ids,
):
    frame_count, row_count, col_count, _ = frames_in.shape
    token_total = frame_count * row_count * col_count * lax.axis_size(ALL)
    both = (frames_in, grad_out)
    below, right, corner = edges(frames_in, grad_out)
    below = shifted(below, -1, 0)
    right = shifted(right, 0, -1)
    corner = shifted(corner, -1, -1)
    rolled = []
    for n, a in enumerate(both):
        upper = jnp.concatenate([a[:, 4:, 4:], right[n]], axis=2)
        lower = jnp.concatenate([below[n][:, :, 4:], corner[n]], axis=2)
        tile = jnp.concatenate([upper, lower], axis=1)
        rolled.append(jnp.concatenate([tile[1:], tile[:1]], axis=0))

    bias, pos_t = gather_bias(pos_index, bias_table.T)
    ids = region_ids.reshape(2, 2, 8, 2, 8).transpose(1, 3, 0, 2, 4).reshape(N_WIN, WIN_TOK)
    me = lax.axis_index("c").reshape(1)
    kept, sent, att, hat, inv, gnorm = main_call(
        rolled[0], rolled[1], norm_gain[None], norm_shift[None], qkv_weight, proj_weight, bias,
        ids, pos_t, me,
    )
    part = add_halves(kept, swap_cores(sent))
    branch, back = token_call(att, hat, inv, gnorm, norm_gain[None], proj_weight)
    plane = ("l", "h", "x")
    part = exchange(part.reshape(lax.axis_size(plane), -1, 128), plane)
    part, branch, back = lax.optimization_barrier((part, branch, back))
    part = exchange(sum_copies(part, lax.axis_size("z")), ("z",))
    flipped = [jnp.concatenate([a[1:], a[:1]], axis=0) for a in (branch, back)]
    above = shifted(jnp.stack([a[:, 12:, :12] for a in flipped]), 1, 0)
    left = shifted(jnp.stack([a[:, :12, 12:] for a in flipped]), 0, 1)
    angle = shifted(jnp.stack([a[:, 12:, 12:] for a in flipped]), 1, 1)
    part, above, left, angle = lax.optimization_barrier((part, above, left, angle))
    outs = []
    for n, a in enumerate(both):
        upper = jnp.concatenate([angle[n], above[n]], axis=2)
        lower = jnp.concatenate([left[n], flipped[n][:, :12, :12]], axis=2)
        moved = jnp.concatenate([upper, lower], axis=1)
        outs.append((a.astype(F32) + moved.astype(F32)).astype(BF16))

    own = exchange(sum_copies(part, lax.axis_size(plane)), plane).reshape(HALF, 128)
    own, outs = lax.optimization_barrier((own, outs))
    other = swap_cores(own)
    grad_qkv, grad_proj, table, gain, shift = unpack(me, own, other, token_total**-0.5)
    return outs[0], outs[1], grad_qkv, grad_proj, table.T, gain.reshape(WIDTH), shift.reshape(WIDTH)


def solution(mesh):
    rows, cols = mesh.devices.shape
    fine = Mesh(mesh.devices.reshape(rows // 4, 2, 2, 2, cols // 2), ALL)
    tile = P(None, ROW, COL, None)
    return jax.shard_map(
        body,
        mesh=fine,
        in_specs=(tile, tile, P(), P(), P(), P(), P(), P(), P(None, ROW, COL)),
        out_specs=(tile, tile, P(), P(), P(), P(), P()),
        check_vma=False,
    )
```

```python
import functools

import jax
import jax.numpy as jnp
from jax import lax
from jax.experimental import pallas as pl
from jax.experimental.pallas import tpu as pltpu
from jax.sharding import Mesh
from jax.sharding import PartitionSpec as P

HEADS = 12
WIN_TOK = 128
TABLE_ROWS = 675
WIDTH = 384
HEAD_DIM = 32
GROUP = 128
N_WIN = 4
TOK = N_WIN * WIN_TOK
NORM_EPS = 1e-05
SCALE = HEAD_DIM**-0.5

ROW_PROJ = 9 * WIDTH
ROW_TABLE = 12 * WIDTH
ROW_NORM = ROW_TABLE + 96
PACK_ROWS = 4864
HALF = PACK_ROWS // 2

F32 = jnp.float32
BF16 = jnp.bfloat16
VMEM_LIMIT = 20 * 1024 * 1024

NN = (((1,), (0,)), ((), ()))
NT = (((1,), (1,)), ((), ()))
TN = (((0,), (0,)), ((), ()))


def mm(a, b, dims):
    return lax.dot_general(a, b, dims, preferred_element_type=F32)


def whole(n):
    return [pl.BlockSpec(memory_space=pltpu.VMEM)] * n


def in_vmem(shape, dtype):
    return pltpu.VMEM(shape, dtype)


def edge_kernel(x_ref, g_ref, below_ref, right_ref, corner_ref, x_s, g_s, sems):
    copies = [
        pltpu.make_async_copy(x_ref, x_s, sems.at[0]),
        pltpu.make_async_copy(g_ref, g_s, sems.at[1]),
    ]
    for copy in copies:
        copy.start()
    for n, ref in enumerate((x_s, g_s)):
        copies[n].wait()
        below_ref[n] = ref[:, 0:4, :, :].astype(F32)[:, :, 4:16, :].astype(BF16)
        right_ref[n] = ref[:, 4:16, 0:4, :]
        corner_ref[n] = ref[:, 0:4, 0:4, :]


def edges(x, g):
    return pl.pallas_call(
        edge_kernel,
        out_shape=(
            in_vmem((2, 2, 4, 12, WIDTH), BF16),
            in_vmem((2, 2, 12, 4, WIDTH), BF16),
            in_vmem((2, 2, 4, 4, WIDTH), BF16),
            in_vmem((2, 16, 16, WIDTH), BF16),
            in_vmem((2, 16, 16, WIDTH), BF16),
        ),
        in_specs=[pl.BlockSpec(memory_space=pltpu.HBM)] * 2,
        out_specs=tuple(whole(5)),
        scratch_shapes=[pltpu.SemaphoreType.DMA((2,))],
        compiler_params=pltpu.CompilerParams(vmem_limit_bytes=VMEM_LIMIT),
        cost_estimate=pl.CostEstimate(flops=0, bytes_accessed=1_200_000, transcendentals=0),
        name="edges",
    )(*(pltpu.with_memory_space_constraint(a, pltpu.HBM) for a in (x, g)))


def bias_kernel(
    pos_ref, table_ref, gain_ref, shift_ref, wqkv_ref, wproj_ref,
    bias_ref, pos_t_ref, gain_v, shift_v, wqkv_v, wproj_v, table_s, sems,
):
    pairs = ((wqkv_ref, wqkv_v), (wproj_ref, wproj_v), (gain_ref, gain_v), (shift_ref, shift_v))
    copies = [pltpu.make_async_copy(a, b, sems.at[n]) for n, (a, b) in enumerate(pairs)]
    for copy in copies:
        copy.start()
    pos_t_ref[...] = pos_ref[...].T
    table_s[...] = jnp.zeros_like(table_s)
    table_s[0:HEADS, 0:TABLE_ROWS] = table_ref[...]

    def rows(step, carry):
        at = pl.multiple_of(step * 8, 8)
        idx = pos_t_ref[pl.ds(at, 8), :]
        low = idx & 127
        high = idx >> 7
        for h in range(HEADS):
            got = None
            for k in range(6):
                chunk = jnp.broadcast_to(table_s[h : h + 1, k * 128 : (k + 1) * 128], (8, 128))
                part = jnp.take_along_axis(chunk, low, axis=1)
                got = part if k == 0 else jnp.where(high == k, part, got)
            bias_ref[h, pl.ds(at, 8), :] = got
        return carry

    lax.fori_loop(0, 16, rows, 0)
    for copy in copies:
        copy.wait()


def gather_bias(pos_index, table_t, *params):
    return pl.pallas_call(
        bias_kernel,
        out_shape=(
            in_vmem((HEADS, WIN_TOK, WIN_TOK), F32),
            in_vmem((WIN_TOK, WIN_TOK), jnp.int32),
        )
        + tuple(in_vmem(a.shape, a.dtype) for a in params),
        in_specs=whole(2) + [pl.BlockSpec(memory_space=pltpu.HBM)] * 4,
        out_specs=tuple(whole(6)),
        scratch_shapes=[pltpu.VMEM((16, 768), F32), pltpu.SemaphoreType.DMA((4,))],
        compiler_params=pltpu.CompilerParams(vmem_limit_bytes=VMEM_LIMIT),
        cost_estimate=pl.CostEstimate(flops=4_000_000, bytes_accessed=900_000, transcendentals=0),
        name="gather_bias",
    )(
        pos_index,
        table_t,
        *(pltpu.with_memory_space_constraint(a, pltpu.HBM) for a in params),
    )


def row_of(ref):
    return jnp.concatenate([ref[k * 128 : (k + 1) * 128].reshape(1, 128) for k in range(3)], axis=1)


def window_tokens(ref, wr, wc):
    block = ref[:, 8 * wr : 8 * wr + 8, :, :].astype(F32)
    return block[:, :, 8 * wc : 8 * wc + 8, :].reshape(WIN_TOK, WIDTH)


def store_tile(ref, tokens):
    for wr in range(2):
        pair = [
            tokens[(2 * wr + wc) * WIN_TOK : (2 * wr + wc + 1) * WIN_TOK].reshape(2, 8, 8, WIDTH)
            for wc in range(2)
        ]
        ref[:, 8 * wr : 8 * wr + 8, :, :] = jnp.concatenate(pair, axis=2).astype(BF16)


def main_kernel(
    x_ref, g_ref, gain_ref, shift_ref, wqkv_ref, wproj_ref, bias_ref, id_ref,
    pos_ref, me_ref, kept_ref, sent_ref, branch_ref, back_ref,
    att_s, hat_s, inv_s, normed_s, g_s, qkv_s, da_s, gqkv_s, table_s, shut_s, pack_ref,
):
    gain = row_of(gain_ref)
    shift = row_of(shift_ref)
    for wr in range(2):
        for wc in range(2):
            at = (2 * wr + wc) * WIN_TOK
            rows = slice(at, at + WIN_TOK)
            x = window_tokens(x_ref, wr, wc)
            centered = x - jnp.mean(x, axis=-1, keepdims=True)
            variance = jnp.mean(centered * centered, axis=-1, keepdims=True)
            inv_std = lax.rsqrt(variance + NORM_EPS)
            x_hat = centered * inv_std
            hat_s[rows, :] = x_hat
            inv_s[rows, :] = jnp.broadcast_to(inv_std, (WIN_TOK, 128))
            normed_s[rows, :] = (x_hat * gain + shift).astype(BF16)
            g_s[rows, :] = window_tokens(g_ref, wr, wc).astype(BF16)
    for p in range(3):
        part = mm(normed_s[...], wqkv_ref[:, p * WIDTH : (p + 1) * WIDTH], NN).astype(BF16)
        for k in range(3):
            qkv_s[3 * p + k] = part[:, k * GROUP : (k + 1) * GROUP]
    part = mm(g_s[...], wproj_ref[...], NT).astype(BF16)
    for k in range(3):
        da_s[k] = part[:, k * GROUP : (k + 1) * GROUP]

    for w in range(N_WIN):
        ids = jnp.broadcast_to(id_ref[w : w + 1, :], (WIN_TOK, WIN_TOK))
        shut_s[w] = jnp.where(ids.T == ids, 0.0, -1e30)
    table_s[...] = jnp.zeros_like(table_s)
    lane = lax.broadcasted_iota(jnp.int32, (WIN_TOK, GROUP), 1) // HEAD_DIM

    def attend(step, carry):
        w = step // 3
        k = step % 3
        rows = pl.ds(pl.multiple_of(w * WIN_TOK, WIN_TOK), WIN_TOK)
        q = qkv_s[k, rows, :]
        key = qkv_s[3 + k, rows, :]
        v = qkv_s[6 + k, rows, :]
        da = da_s[k, rows, :]
        shut = shut_s[w]
        zero = jnp.zeros_like(q)
        heads = []
        for h in range(4):
            mine = lane == h
            heads.append(tuple(jnp.where(mine, a, zero) for a in (q, key, v, da)))
        probs, grads = [], []
        q_all, key_all, v_all, da_all = (
            jnp.concatenate([heads[h][n] for h in range(4)], axis=0) for n in range(4)
        )
        score_all = mm(key_all, q, NT)
        grad_all = mm(v_all, da, NT)
        for h in range(4):
            _, key_h, v_h, _ = heads[h]
            score = score_all[128 * h : 128 * h + 128] * SCALE + bias_ref[4 * k + h] + shut
            top = jnp.max(score, axis=0, keepdims=True)
            e = jnp.exp(score - top)
            prob = e * (1.0 / jnp.sum(e, axis=0, keepdims=True))
            grad_prob = grad_all[128 * h : 128 * h + 128]
            inner = jnp.sum(prob * grad_prob, axis=0, keepdims=True)
            grad_score = prob * (grad_prob - inner)
            table_s[4 * k + h] += grad_score
            probs.append(prob.astype(BF16))
            grads.append((grad_score * SCALE).astype(BF16))
        prob_rows = jnp.concatenate(probs, axis=0)
        grad_rows = jnp.concatenate(grads, axis=0)
        att_s[k, rows, :] = mm(prob_rows, v_all, TN).astype(BF16)
        gqkv_s[k, rows, :] = mm(grad_rows, key_all, TN).astype(BF16)
        gqkv_s[3 + k, rows, :] = mm(jnp.concatenate(grads, axis=1), q_all, NN).astype(BF16)
        gqkv_s[6 + k, rows, :] = mm(jnp.concatenate(probs, axis=1), da_all, NN).astype(BF16)
        return carry

    lax.fori_loop(0, 12, attend, 0, unroll=6)

    attended = jnp.concatenate([att_s[k] for k in range(3)], axis=1)
    store_tile(branch_ref, mm(attended, wproj_ref[...], NN))
    grad_proj = mm(attended, g_s[...], TN)
    for k in range(3):
        at = ROW_PROJ + k * WIDTH
        pack_ref[at : at + WIDTH, :] = grad_proj[:, k * GROUP : (k + 1) * GROUP].astype(BF16)

    grad_normed = None
    for p in range(3):
        grad_part = jnp.concatenate([gqkv_s[3 * p + k] for k in range(3)], axis=1)
        grad_w = mm(normed_s[...], grad_part, TN)
        for k in range(3):
            at = (3 * p + k) * WIDTH
            pack_ref[at : at + WIDTH, :] = grad_w[:, k * GROUP : (k + 1) * GROUP].astype(BF16)
        term = mm(grad_part, wqkv_ref[:, p * WIDTH : (p + 1) * WIDTH], NT)
        grad_normed = term if p == 0 else grad_normed + term
    x_hat = hat_s[...]
    grad_gain = jnp.sum(grad_normed * x_hat, axis=0, keepdims=True)
    grad_shift = jnp.sum(grad_normed, axis=0, keepdims=True)
    scaled = grad_normed * gain
    store_tile(
        back_ref,
        inv_s[:, 0:1]
        * (
            scaled
            - jnp.mean(scaled, axis=-1, keepdims=True)
            - x_hat * jnp.mean(scaled * x_hat, axis=-1, keepdims=True)
        ),
    )

    low_bins = lax.broadcasted_iota(jnp.int32, (128, WIN_TOK), 0)

    def bins(step, acc):
        at = pl.multiple_of(step * 8, 8)
        index = pos_ref[pl.ds(at, 8), :]
        block = jnp.swapaxes(table_s[:, pl.ds(at, 8), :], 0, 1)
        for n in range(0, 8, 2):
            left, right = [], []
            for j in (n, n + 1):
                idx = index[j : j + 1]
                high = idx >> 7
                terms = block[j]
                left.append(
                    jnp.concatenate([jnp.where(high == a, terms, 0.0) for a in range(6)], axis=0)
                )
                right.append(jnp.where(low_bins == (idx & 127), 1.0, 0.0))
            acc = acc + mm(
                jnp.concatenate(left, axis=1).astype(BF16),
                jnp.concatenate(right, axis=1).astype(BF16),
                NT,
            )
        return acc

    table = lax.fori_loop(0, WIN_TOK // 8, bins, jnp.zeros((96, 128), F32), unroll=4)
    pack_ref[ROW_TABLE : ROW_TABLE + 96, :] = table.astype(BF16)
    norm_rows = [a[:, k * 128 : (k + 1) * 128] for a in (grad_gain, grad_shift) for k in range(3)]
    norm_rows.append(jnp.zeros((10, 128), F32))
    pack_ref[ROW_NORM : ROW_NORM + 16, :] = jnp.concatenate(norm_rows, axis=0).astype(BF16)
    pack_ref[ROW_NORM + 16 :, :] = jnp.zeros((PACK_ROWS - ROW_NORM - 16, 128), BF16)
    me = me_ref[0]
    kept_ref[...] = pack_ref[pl.ds(pl.multiple_of(me * HALF, HALF), HALF), :]
    sent_ref[...] = pack_ref[pl.ds(pl.multiple_of((1 - me) * HALF, HALF), HALF), :]


def main_call(*args):
    return pl.pallas_call(
        main_kernel,
        out_shape=(
            in_vmem((HALF, 128), BF16),
            in_vmem((HALF, 128), BF16),
            in_vmem((2, 16, 16, WIDTH), BF16),
            in_vmem((2, 16, 16, WIDTH), BF16),
        ),
        in_specs=whole(len(args) - 1) + [pl.BlockSpec(memory_space=pltpu.SMEM)],
        out_specs=tuple(whole(4)),
        scratch_shapes=[
            pltpu.VMEM((3, TOK, GROUP), BF16),
            pltpu.VMEM((TOK, WIDTH), F32),
            pltpu.VMEM((TOK, 128), F32),
            pltpu.VMEM((TOK, WIDTH), BF16),
            pltpu.VMEM((TOK, WIDTH), BF16),
            pltpu.VMEM((9, TOK, GROUP), BF16),
            pltpu.VMEM((3, TOK, GROUP), BF16),
            pltpu.VMEM((9, TOK, GROUP), BF16),
            pltpu.VMEM((16, WIN_TOK, WIN_TOK), F32),
            pltpu.VMEM((N_WIN, WIN_TOK, WIN_TOK), F32),
            pltpu.VMEM((PACK_ROWS, 128), BF16),
        ],
        compiler_params=pltpu.CompilerParams(vmem_limit_bytes=VMEM_LIMIT),
        cost_estimate=pl.CostEstimate(
            flops=4_000_000_000, bytes_accessed=6_000_000, transcendentals=800_000
        ),
        name="block_pass",
    )(*args)


def unpack_kernel(
    factor, me_ref, own_ref, other_ref, qkv_ref, proj_ref, table_ref, gain_ref, shift_ref, pack_ref
):
    me = me_ref[0]
    pack_ref[pl.ds(pl.multiple_of(me * HALF, HALF), HALF), :] = own_ref[...]
    pack_ref[pl.ds(pl.multiple_of((1 - me) * HALF, HALF), HALF), :] = other_ref[...]
    for k in range(12):
        block = pack_ref[k * WIDTH : (k + 1) * WIDTH, :].astype(F32) * factor
        if k < 9:
            qkv_ref[:, k * 128 : (k + 1) * 128] = block
        else:
            proj_ref[:, (k - 9) * 128 : (k - 8) * 128] = block
    table = pack_ref[ROW_TABLE : ROW_TABLE + 96, :].astype(F32) * factor
    wide = jnp.concatenate([table[16 * a : 16 * a + 16] for a in range(6)], axis=1)
    table_ref[...] = wide[0:HEADS, 0:TABLE_ROWS]
    norm = pack_ref[ROW_NORM : ROW_NORM + 16, :].astype(F32) * factor
    for n, ref in enumerate((gain_ref, shift_ref)):
        for k in range(3):
            ref[k * 128 : (k + 1) * 128] = norm[3 * n + k]


def unpack(me, own, other, factor):
    return pl.pallas_call(
        functools.partial(unpack_kernel, factor),
        out_shape=(
            jax.ShapeDtypeStruct((WIDTH, 3 * WIDTH), F32),
            jax.ShapeDtypeStruct((WIDTH, WIDTH), F32),
            jax.ShapeDtypeStruct((HEADS, TABLE_ROWS), F32),
            jax.ShapeDtypeStruct((WIDTH,), F32),
            jax.ShapeDtypeStruct((WIDTH,), F32),
        ),
        in_specs=[pl.BlockSpec(memory_space=pltpu.SMEM)] + whole(2),
        out_specs=tuple(whole(5)),
        scratch_shapes=[pltpu.VMEM((PACK_ROWS, 128), BF16)],
        compiler_params=pltpu.CompilerParams(vmem_limit_bytes=VMEM_LIMIT),
        cost_estimate=pl.CostEstimate(flops=600_000, bytes_accessed=3_600_000, transcendentals=0),
        name="unpack_sums",
    )(me, own, other)


def add_kernel(a_ref, b_ref, out_ref):
    out_ref[...] = (a_ref[...].astype(F32) + b_ref[...].astype(F32)).astype(BF16)


def add_halves(a, b):
    return pl.pallas_call(
        add_kernel,
        out_shape=in_vmem((HALF, 128), BF16),
        in_specs=whole(2),
        out_specs=pl.BlockSpec(memory_space=pltpu.VMEM),
        compiler_params=pltpu.CompilerParams(vmem_limit_bytes=VMEM_LIMIT),
        cost_estimate=pl.CostEstimate(flops=300_000, bytes_accessed=1_800_000, transcendentals=0),
        name="add_halves",
    )(a, b)


def copies_kernel(parts_ref, out_ref):
    total = parts_ref[0].astype(F32)
    for n in range(1, parts_ref.shape[0]):
        total += parts_ref[n].astype(F32)
    total = total.astype(BF16)
    for n in range(out_ref.shape[0]):
        out_ref[n] = total


def sum_copies(parts, count):
    return pl.pallas_call(
        copies_kernel,
        out_shape=in_vmem((count,) + parts.shape[1:], BF16),
        in_specs=whole(1),
        out_specs=pl.BlockSpec(memory_space=pltpu.VMEM),
        compiler_params=pltpu.CompilerParams(vmem_limit_bytes=VMEM_LIMIT),
        cost_estimate=pl.CostEstimate(flops=300_000, bytes_accessed=1_200_000, transcendentals=0),
        name="sum_copies",
    )(parts)


ROW = ("z", "l", "c")
COL = ("h", "x")
ALL = ROW + COL


def shifted(value, row_step, col_step):
    rows = lax.axis_size(ROW)
    cols = lax.axis_size(COL)
    pairs = [
        (r * cols + c, ((r + row_step) % rows) * cols + (c + col_step) % cols)
        for r in range(rows)
        for c in range(cols)
    ]
    return lax.ppermute(value, ALL, pairs)


def exchange(parts, axes):
    return lax.all_to_all(parts, axes, 0, 0)


def swap_cores(value):
    count = lax.axis_size(ALL)
    cols = lax.axis_size(COL)
    return lax.ppermute(value, ALL, [(i, i ^ cols) for i in range(count)])


def body(
    frames_in, grad_out, norm_gain, norm_shift, qkv_weight, proj_weight, bias_table, pos_index,
    region_ids,
):
    frame_count, row_count, col_count, _ = frames_in.shape
    token_total = frame_count * row_count * col_count * lax.axis_size(ALL)
    both = (frames_in, grad_out)
    below, right, corner, x_tile, g_tile = edges(frames_in, grad_out)
    below = shifted(below, -1, 0)
    right = shifted(right, 0, -1)
    corner = shifted(corner, -1, -1)
    rolled = []
    for n, a in enumerate((x_tile, g_tile)):
        upper = jnp.concatenate([a[:, 4:, 4:], right[n]], axis=2)
        lower = jnp.concatenate([below[n], corner[n]], axis=2)
        tile = jnp.concatenate([upper, lower], axis=1)
        rolled.append(jnp.concatenate([tile[1:], tile[:1]], axis=0))

    bias, pos_t, gain_v, shift_v, wqkv_v, wproj_v = gather_bias(
        pos_index, bias_table.T, norm_gain, norm_shift, qkv_weight, proj_weight
    )
    ids = region_ids.reshape(2, 2, 8, 2, 8).transpose(1, 3, 0, 2, 4).reshape(N_WIN, WIN_TOK)
    me = lax.axis_index("c").reshape(1)
    kept, sent, branch, back = main_call(
        rolled[0], rolled[1], gain_v, shift_v, wqkv_v, wproj_v, bias,
        ids, pos_t, me,
    )
    part = add_halves(kept, swap_cores(sent))
    plane = ("l", "h", "x")
    part = exchange(part.reshape(lax.axis_size(plane), -1, 128), plane)
    part, branch, back = lax.optimization_barrier((part, branch, back))
    part = exchange(sum_copies(part, lax.axis_size("z")), ("z",))
    flipped = [jnp.concatenate([a[1:], a[:1]], axis=0) for a in (branch, back)]
    above = shifted(jnp.stack([a[:, 12:, :12] for a in flipped]), 1, 0)
    left = shifted(jnp.stack([a[:, :12, 12:] for a in flipped]), 0, 1)
    angle = shifted(jnp.stack([a[:, 12:, 12:] for a in flipped]), 1, 1)
    part, above, left, angle = lax.optimization_barrier((part, above, left, angle))
    outs = []
    for n, a in enumerate(both):
        upper = jnp.concatenate([angle[n], above[n]], axis=2)
        lower = jnp.concatenate([left[n], flipped[n][:, :12, :12]], axis=2)
        moved = jnp.concatenate([upper, lower], axis=1)
        outs.append((a.astype(F32) + moved.astype(F32)).astype(BF16))

    own = exchange(sum_copies(part, lax.axis_size(plane)), plane).reshape(HALF, 128)
    own, outs = lax.optimization_barrier((own, outs))
    other = swap_cores(own)
    grad_qkv, grad_proj, table, gain, shift = unpack(me, own, other, token_total**-0.5)
    return outs[0], outs[1], grad_qkv, grad_proj, table.T, gain, shift


def solution(mesh):
    rows, cols = mesh.devices.shape
    fine = Mesh(mesh.devices.reshape(rows // 4, 2, 2, 2, cols // 2), ALL)
    tile = P(None, ROW, COL, None)
    return jax.shard_map(
        body,
        mesh=fine,
        in_specs=(tile, tile, P(), P(), P(), P(), P(), P(), P(None, ROW, COL)),
        out_specs=(tile, tile, P(), P(), P(), P(), P()),
        check_vma=False,
    )
```

```python
import functools

import jax
import jax.numpy as jnp
from jax import lax
from jax.experimental import pallas as pl
from jax.experimental.pallas import tpu as pltpu
from jax.sharding import Mesh
from jax.sharding import PartitionSpec as P

HEADS = 12
WIN_TOK = 128
TABLE_ROWS = 675
WIDTH = 384
HEAD_DIM = 32
GROUP = 128
N_WIN = 4
TOK = N_WIN * WIN_TOK
NORM_EPS = 1e-05
SCALE = HEAD_DIM**-0.5

ROW_PROJ = 9 * WIDTH
ROW_TABLE = 12 * WIDTH
ROW_NORM = ROW_TABLE + 96
PACK_ROWS = 4864
HALF = PACK_ROWS // 2

F32 = jnp.float32
BF16 = jnp.bfloat16
VMEM_LIMIT = 20 * 1024 * 1024

NN = (((1,), (0,)), ((), ()))
NT = (((1,), (1,)), ((), ()))
TN = (((0,), (0,)), ((), ()))


def mm(a, b, dims):
    return lax.dot_general(a, b, dims, preferred_element_type=F32)


def whole(n):
    return [pl.BlockSpec(memory_space=pltpu.VMEM)] * n


def in_vmem(shape, dtype):
    return pltpu.VMEM(shape, dtype)


def edge_kernel(
    x_ref, g_ref, pos_ref, table_ref, id_ref,
    below_ref, right_ref, corner_ref, x_s, g_s, pos_s, table_s, id_s, sems,
):
    pairs = (
        (x_ref, x_s), (g_ref, g_s), (pos_ref, pos_s), (table_ref, table_s), (id_ref, id_s),
    )
    copies = [pltpu.make_async_copy(a, b, sems.at[n]) for n, (a, b) in enumerate(pairs)]
    for copy in copies:
        copy.start()
    for n, ref in enumerate((x_s, g_s)):
        copies[n].wait()
        below_ref[n] = ref[:, 0:4, :, :].astype(F32)[:, :, 4:16, :].astype(BF16)
        right_ref[n] = ref[:, 4:16, 0:4, :]
        corner_ref[n] = ref[:, 0:4, 0:4, :]
    for copy in copies[2:]:
        copy.wait()


def edges(*args):
    return pl.pallas_call(
        edge_kernel,
        out_shape=(
            in_vmem((2, 2, 4, 12, WIDTH), BF16),
            in_vmem((2, 2, 12, 4, WIDTH), BF16),
            in_vmem((2, 2, 4, 4, WIDTH), BF16),
        )
        + tuple(in_vmem(a.shape, a.dtype) for a in args),
        in_specs=[pl.BlockSpec(memory_space=pltpu.HBM)] * 5,
        out_specs=tuple(whole(8)),
        scratch_shapes=[pltpu.SemaphoreType.DMA((5,))],
        compiler_params=pltpu.CompilerParams(vmem_limit_bytes=VMEM_LIMIT),
        cost_estimate=pl.CostEstimate(flops=0, bytes_accessed=1_200_000, transcendentals=0),
        name="edges",
    )(*(pltpu.with_memory_space_constraint(a, pltpu.HBM) for a in args))


def bias_kernel(
    pos_ref, table_ref, x_ref, g_ref, id_ref, gain_ref, shift_ref, wqkv_ref, wproj_ref,
    bias_ref, pos_t_ref, hat_ref, inv_ref, normed_ref, g0_ref, att_ref, gqkv_ref, sums_ref,
    gain_v, shift_v, wqkv_v, wproj_v, table_s, qkv_s, da_s, sems,
):
    pairs = ((wqkv_ref, wqkv_v), (wproj_ref, wproj_v), (gain_ref, gain_v), (shift_ref, shift_v))
    copies = [pltpu.make_async_copy(a, b, sems.at[n]) for n, (a, b) in enumerate(pairs)]
    for copy in copies:
        copy.start()
    pos_t_ref[...] = pos_ref[...].T
    table_s[...] = jnp.zeros_like(table_s)
    table_s[0:HEADS, 0:TABLE_ROWS] = table_ref[...]

    def rows(step, carry):
        at = pl.multiple_of(step * 8, 8)
        idx = pos_t_ref[pl.ds(at, 8), :]
        low = idx & 127
        high = idx >> 7
        for h in range(HEADS):
            got = None
            for k in range(6):
                chunk = jnp.broadcast_to(table_s[h : h + 1, k * 128 : (k + 1) * 128], (8, 128))
                part = jnp.take_along_axis(chunk, low, axis=1)
                got = part if k == 0 else jnp.where(high == k, part, got)
            bias_ref[h, pl.ds(at, 8), :] = got
        return carry

    lax.fori_loop(0, 16, rows, 0)
    for copy in copies:
        copy.wait()
    sums_ref[...] = jnp.zeros_like(sums_ref)
    first = slice(0, WIN_TOK)
    x = window_tokens(0, x_ref, None, None, None, 0, 0)
    g = window_tokens(1, g_ref, None, None, None, 0, 0)
    normalize(x, g, row_of(gain_v), row_of(shift_v), first, hat_ref, inv_ref, normed_ref, g0_ref)
    project(first, normed_ref, g0_ref, wqkv_v, wproj_v, qkv_s, da_s)
    shut = shut_pairs(id_ref, 0)
    for k in range(3):
        attend(k, first, shut, bias_ref, qkv_s, da_s, att_ref, gqkv_ref, sums_ref)


def gather_bias(pos_index, table_t, x, g, ids, *params):
    return pl.pallas_call(
        bias_kernel,
        out_shape=(
            in_vmem((HEADS, WIN_TOK, WIN_TOK), F32),
            in_vmem((WIN_TOK, WIN_TOK), jnp.int32),
            in_vmem((WIN_TOK, WIDTH), F32),
            in_vmem((WIN_TOK, 128), F32),
            in_vmem((WIN_TOK, WIDTH), BF16),
            in_vmem((WIN_TOK, WIDTH), BF16),
            in_vmem((3, WIN_TOK, GROUP), BF16),
            in_vmem((9, WIN_TOK, GROUP), BF16),
            in_vmem((16, WIN_TOK, WIN_TOK), F32),
        )
        + tuple(in_vmem(a.shape, a.dtype) for a in params),
        in_specs=whole(5) + [pl.BlockSpec(memory_space=pltpu.HBM)] * 4,
        out_specs=tuple(whole(13)),
        scratch_shapes=[
            pltpu.VMEM((16, 768), F32),
            pltpu.VMEM((9, WIN_TOK, GROUP), BF16),
            pltpu.VMEM((3, WIN_TOK, GROUP), BF16),
            pltpu.SemaphoreType.DMA((4,)),
        ],
        compiler_params=pltpu.CompilerParams(vmem_limit_bytes=VMEM_LIMIT),
        cost_estimate=pl.CostEstimate(flops=4_000_000, bytes_accessed=900_000, transcendentals=0),
        name="gather_bias",
    )(
        pos_index,
        table_t,
        x,
        g,
        ids,
        *(pltpu.with_memory_space_constraint(a, pltpu.HBM) for a in params),
    )


def row_of(ref):
    return jnp.concatenate([ref[k * 128 : (k + 1) * 128].reshape(1, 128) for k in range(3)], axis=1)


def window_tokens(n, tile_ref, below_ref, right_ref, corner_ref, wr, wc):
    def columns(rows, side):
        if wc == 0:
            return rows[:, :, 0:8, :]
        return jnp.concatenate([rows[:, :, 8:12, :], side().astype(F32)], axis=2)

    top = 4 + 8 * wr
    own = 8 - 4 * wr
    rows = columns(
        tile_ref[:, top : top + own, :, :].astype(F32)[:, :, 4:16, :],
        lambda: right_ref[n, :, top - 4 : top - 4 + own, :, :],
    )
    if wr == 1:
        lower = columns(below_ref[n].astype(F32), lambda: corner_ref[n])
        rows = jnp.concatenate([rows, lower], axis=1)
    return jnp.concatenate([rows[1:], rows[:1]], axis=0).reshape(WIN_TOK, WIDTH)


def store_tile(ref, tokens):
    for wr in range(2):
        pair = [
            tokens[(2 * wr + wc) * WIN_TOK : (2 * wr + wc + 1) * WIN_TOK].reshape(2, 8, 8, WIDTH)
            for wc in range(2)
        ]
        ref[:, 8 * wr : 8 * wr + 8, :, :] = jnp.concatenate(pair, axis=2).astype(BF16)


def normalize(x, g, gain, shift, rows, hat_s, inv_s, normed_s, g_s):
    centered = x - jnp.mean(x, axis=-1, keepdims=True)
    variance = jnp.mean(centered * centered, axis=-1, keepdims=True)
    inv_std = lax.rsqrt(variance + NORM_EPS)
    x_hat = centered * inv_std
    hat_s[rows, :] = x_hat
    inv_s[rows, :] = jnp.broadcast_to(inv_std, (WIN_TOK, 128))
    normed_s[rows, :] = (x_hat * gain + shift).astype(BF16)
    g_s[rows, :] = g.astype(BF16)


def shut_pairs(id_ref, w):
    ids = jnp.broadcast_to(id_ref[w : w + 1, :], (WIN_TOK, WIN_TOK))
    return jnp.where(ids.T == ids, 0.0, -1e30)


def project(rows, normed_s, g_s, wqkv_ref, wproj_ref, qkv_s, da_s):
    for p in range(3):
        part = mm(normed_s[rows, :], wqkv_ref[:, p * WIDTH : (p + 1) * WIDTH], NN).astype(BF16)
        for k in range(3):
            qkv_s[3 * p + k, rows, :] = part[:, k * GROUP : (k + 1) * GROUP]
    part = mm(g_s[rows, :], wproj_ref[...], NT).astype(BF16)
    for k in range(3):
        da_s[k, rows, :] = part[:, k * GROUP : (k + 1) * GROUP]


def attend(k, rows, shut, bias_ref, qkv_s, da_s, att_s, gqkv_s, table_s):
    lane = lax.broadcasted_iota(jnp.int32, (WIN_TOK, GROUP), 1) // HEAD_DIM
    q = qkv_s[k, rows, :]
    key = qkv_s[3 + k, rows, :]
    v = qkv_s[6 + k, rows, :]
    da = da_s[k, rows, :]
    zero = jnp.zeros_like(q)
    q_all, key_all, v_all, da_all = (
        jnp.concatenate([jnp.where(lane == h, a, zero) for h in range(4)], axis=0)
        for a in (q, key, v, da)
    )
    score_all = mm(key_all, q, NT)
    grad_all = mm(v_all, da, NT)
    probs, grads = [], []
    for h in range(4):
        score = score_all[128 * h : 128 * h + 128] * SCALE + bias_ref[4 * k + h] + shut
        top = jnp.max(score, axis=0, keepdims=True)
        e = jnp.exp(score - top)
        prob = e * (1.0 / jnp.sum(e, axis=0, keepdims=True))
        grad_prob = grad_all[128 * h : 128 * h + 128]
        inner = jnp.sum(prob * grad_prob, axis=0, keepdims=True)
        grad_score = prob * (grad_prob - inner)
        table_s[4 * k + h] += grad_score
        probs.append(prob.astype(BF16))
        grads.append((grad_score * SCALE).astype(BF16))
    prob_rows = jnp.concatenate(probs, axis=0)
    grad_rows = jnp.concatenate(grads, axis=0)
    att_s[k, rows, :] = mm(prob_rows, v_all, TN).astype(BF16)
    gqkv_s[k, rows, :] = mm(grad_rows, key_all, TN).astype(BF16)
    gqkv_s[3 + k, rows, :] = mm(jnp.concatenate(grads, axis=1), q_all, NN).astype(BF16)
    gqkv_s[6 + k, rows, :] = mm(jnp.concatenate(probs, axis=1), da_all, NN).astype(BF16)


def main_kernel(
    x_ref, g_ref, below_ref, right_ref, corner_ref, gain_ref, shift_ref, wqkv_ref, wproj_ref, bias_ref, id_ref,
    pos_ref, hat0_ref, inv0_ref, normed0_ref, g0_ref, att0_ref, gqkv0_ref, table0_ref,
    me_ref, kept_ref, sent_ref, branch_ref, back_ref,
    att_s, hat_s, inv_s, normed_s, g_s, qkv_s, da_s, gqkv_s, table_s, shut_s, pack_ref,
):
    gain = row_of(gain_ref)
    shift = row_of(shift_ref)
    edge_refs = (below_ref, right_ref, corner_ref)
    first = slice(0, WIN_TOK)
    hat_s[first, :] = hat0_ref[...]
    inv_s[first, :] = inv0_ref[...]
    normed_s[first, :] = normed0_ref[...]
    g_s[first, :] = g0_ref[...]
    att_s[:, first, :] = att0_ref[...]
    gqkv_s[:, first, :] = gqkv0_ref[...]
    table_s[...] = table0_ref[...]
    for w in range(1, N_WIN):
        x = window_tokens(0, x_ref, *edge_refs, w // 2, w % 2)
        g = window_tokens(1, g_ref, *edge_refs, w // 2, w % 2)
        rows = slice(w * WIN_TOK, (w + 1) * WIN_TOK)
        normalize(x, g, gain, shift, rows, hat_s, inv_s, normed_s, g_s)
        shut_s[w] = shut_pairs(id_ref, w)
    project(slice(WIN_TOK, TOK), normed_s, g_s, wqkv_ref, wproj_ref, qkv_s, da_s)

    def step_of(step, carry):
        w = (step + 3) // 3
        rows = pl.ds(pl.multiple_of(w * WIN_TOK, WIN_TOK), WIN_TOK)
        attend(step % 3, rows, shut_s[w], bias_ref, qkv_s, da_s, att_s, gqkv_s, table_s)
        return carry

    lax.fori_loop(0, 9, step_of, 0, unroll=3)

    attended = jnp.concatenate([att_s[k] for k in range(3)], axis=1)
    store_tile(branch_ref, mm(attended, wproj_ref[...], NN))
    grad_proj = mm(attended, g_s[...], TN)
    for k in range(3):
        at = ROW_PROJ + k * WIDTH
        pack_ref[at : at + WIDTH, :] = grad_proj[:, k * GROUP : (k + 1) * GROUP].astype(BF16)

    grad_normed = None
    for p in range(3):
        grad_part = jnp.concatenate([gqkv_s[3 * p + k] for k in range(3)], axis=1)
        grad_w = mm(normed_s[...], grad_part, TN)
        for k in range(3):
            at = (3 * p + k) * WIDTH
            pack_ref[at : at + WIDTH, :] = grad_w[:, k * GROUP : (k + 1) * GROUP].astype(BF16)
        term = mm(grad_part, wqkv_ref[:, p * WIDTH : (p + 1) * WIDTH], NT)
        grad_normed = term if p == 0 else grad_normed + term
    x_hat = hat_s[...]
    grad_gain = jnp.sum(grad_normed * x_hat, axis=0, keepdims=True)
    grad_shift = jnp.sum(grad_normed, axis=0, keepdims=True)
    scaled = grad_normed * gain
    store_tile(
        back_ref,
        inv_s[:, 0:1]
        * (
            scaled
            - jnp.mean(scaled, axis=-1, keepdims=True)
            - x_hat * jnp.mean(scaled * x_hat, axis=-1, keepdims=True)
        ),
    )

    low_bins = lax.broadcasted_iota(jnp.int32, (128, WIN_TOK), 0)

    def bins(step, acc):
        at = pl.multiple_of(step * 8, 8)
        index = pos_ref[pl.ds(at, 8), :]
        block = jnp.swapaxes(table_s[:, pl.ds(at, 8), :], 0, 1)
        for n in range(0, 8, 2):
            left, right = [], []
            for j in (n, n + 1):
                idx = index[j : j + 1]
                high = idx >> 7
                terms = block[j]
                left.append(
                    jnp.concatenate([jnp.where(high == a, terms, 0.0) for a in range(6)], axis=0)
                )
                right.append(jnp.where(low_bins == (idx & 127), 1.0, 0.0))
            acc = acc + mm(
                jnp.concatenate(left, axis=1).astype(BF16),
                jnp.concatenate(right, axis=1).astype(BF16),
                NT,
            )
        return acc

    table = lax.fori_loop(0, WIN_TOK // 8, bins, jnp.zeros((96, 128), F32), unroll=4)
    pack_ref[ROW_TABLE : ROW_TABLE + 96, :] = table.astype(BF16)
    norm_rows = [a[:, k * 128 : (k + 1) * 128] for a in (grad_gain, grad_shift) for k in range(3)]
    norm_rows.append(jnp.zeros((10, 128), F32))
    pack_ref[ROW_NORM : ROW_NORM + 16, :] = jnp.concatenate(norm_rows, axis=0).astype(BF16)
    pack_ref[ROW_NORM + 16 :, :] = jnp.zeros((PACK_ROWS - ROW_NORM - 16, 128), BF16)
    me = me_ref[0]
    kept_ref[...] = pack_ref[pl.ds(pl.multiple_of(me * HALF, HALF), HALF), :]
    sent_ref[...] = pack_ref[pl.ds(pl.multiple_of((1 - me) * HALF, HALF), HALF), :]


def main_call(*args):
    return pl.pallas_call(
        main_kernel,
        out_shape=(
            in_vmem((HALF, 128), BF16),
            in_vmem((HALF, 128), BF16),
            in_vmem((2, 16, 16, WIDTH), BF16),
            in_vmem((2, 16, 16, WIDTH), BF16),
        ),
        in_specs=whole(len(args) - 1) + [pl.BlockSpec(memory_space=pltpu.SMEM)],
        out_specs=tuple(whole(4)),
        scratch_shapes=[
            pltpu.VMEM((3, TOK, GROUP), BF16),
            pltpu.VMEM((TOK, WIDTH), F32),
            pltpu.VMEM((TOK, 128), F32),
            pltpu.VMEM((TOK, WIDTH), BF16),
            pltpu.VMEM((TOK, WIDTH), BF16),
            pltpu.VMEM((9, TOK, GROUP), BF16),
            pltpu.VMEM((3, TOK, GROUP), BF16),
            pltpu.VMEM((9, TOK, GROUP), BF16),
            pltpu.VMEM((16, WIN_TOK, WIN_TOK), F32),
            pltpu.VMEM((N_WIN, WIN_TOK, WIN_TOK), F32),
            pltpu.VMEM((PACK_ROWS, 128), BF16),
        ],
        compiler_params=pltpu.CompilerParams(vmem_limit_bytes=VMEM_LIMIT),
        cost_estimate=pl.CostEstimate(
            flops=4_000_000_000, bytes_accessed=6_000_000, transcendentals=800_000
        ),
        name="block_pass",
    )(*args)


def unpack_kernel(
    factor, me_ref, own_ref, other_ref, qkv_ref, proj_ref, table_ref, gain_ref, shift_ref, pack_ref
):
    me = me_ref[0]
    pack_ref[pl.ds(pl.multiple_of(me * HALF, HALF), HALF), :] = own_ref[...]
    pack_ref[pl.ds(pl.multiple_of((1 - me) * HALF, HALF), HALF), :] = other_ref[...]
    for k in range(12):
        block = pack_ref[k * WIDTH : (k + 1) * WIDTH, :].astype(F32) * factor
        if k < 9:
            qkv_ref[:, k * 128 : (k + 1) * 128] = block
        else:
            proj_ref[:, (k - 9) * 128 : (k - 8) * 128] = block
    table = pack_ref[ROW_TABLE : ROW_TABLE + 96, :].astype(F32) * factor
    wide = jnp.concatenate([table[16 * a : 16 * a + 16] for a in range(6)], axis=1)
    table_ref[...] = wide[0:HEADS, 0:TABLE_ROWS]
    norm = pack_ref[ROW_NORM : ROW_NORM + 16, :].astype(F32) * factor
    for n, ref in enumerate((gain_ref, shift_ref)):
        for k in range(3):
            ref[k * 128 : (k + 1) * 128] = norm[3 * n + k]


def unpack(me, own, other, factor):
    return pl.pallas_call(
        functools.partial(unpack_kernel, factor),
        out_shape=(
            jax.ShapeDtypeStruct((WIDTH, 3 * WIDTH), F32),
            jax.ShapeDtypeStruct((WIDTH, WIDTH), F32),
            jax.ShapeDtypeStruct((HEADS, TABLE_ROWS), F32),
            jax.ShapeDtypeStruct((WIDTH,), F32),
            jax.ShapeDtypeStruct((WIDTH,), F32),
        ),
        in_specs=[pl.BlockSpec(memory_space=pltpu.SMEM)] + whole(2),
        out_specs=tuple(whole(5)),
        scratch_shapes=[pltpu.VMEM((PACK_ROWS, 128), BF16)],
        compiler_params=pltpu.CompilerParams(vmem_limit_bytes=VMEM_LIMIT),
        cost_estimate=pl.CostEstimate(flops=600_000, bytes_accessed=3_600_000, transcendentals=0),
        name="unpack_sums",
    )(me, own, other)


def add_kernel(a_ref, b_ref, out_ref):
    out_ref[...] = (a_ref[...].astype(F32) + b_ref[...].astype(F32)).astype(BF16)


def add_halves(a, b):
    return pl.pallas_call(
        add_kernel,
        out_shape=in_vmem((HALF, 128), BF16),
        in_specs=whole(2),
        out_specs=pl.BlockSpec(memory_space=pltpu.VMEM),
        compiler_params=pltpu.CompilerParams(vmem_limit_bytes=VMEM_LIMIT),
        cost_estimate=pl.CostEstimate(flops=300_000, bytes_accessed=1_800_000, transcendentals=0),
        name="add_halves",
    )(a, b)


def copies_kernel(parts_ref, out_ref):
    total = parts_ref[0].astype(F32)
    for n in range(1, parts_ref.shape[0]):
        total += parts_ref[n].astype(F32)
    total = total.astype(BF16)
    for n in range(out_ref.shape[0]):
        out_ref[n] = total


def sum_copies(parts, count):
    return pl.pallas_call(
        copies_kernel,
        out_shape=in_vmem((count,) + parts.shape[1:], BF16),
        in_specs=whole(1),
        out_specs=pl.BlockSpec(memory_space=pltpu.VMEM),
        compiler_params=pltpu.CompilerParams(vmem_limit_bytes=VMEM_LIMIT),
        cost_estimate=pl.CostEstimate(flops=300_000, bytes_accessed=1_200_000, transcendentals=0),
        name="sum_copies",
    )(parts)


ROW = ("z", "l", "c")
COL = ("h", "x")
ALL = ROW + COL


def shifted(value, row_step, col_step):
    rows = lax.axis_size(ROW)
    cols = lax.axis_size(COL)
    pairs = [
        (r * cols + c, ((r + row_step) % rows) * cols + (c + col_step) % cols)
        for r in range(rows)
        for c in range(cols)
    ]
    return lax.ppermute(value, ALL, pairs)


def exchange(parts, axes):
    return lax.all_to_all(parts, axes, 0, 0)


def swap_cores(value):
    count = lax.axis_size(ALL)
    cols = lax.axis_size(COL)
    return lax.ppermute(value, ALL, [(i, i ^ cols) for i in range(count)])


def body(
    frames_in, grad_out, norm_gain, norm_shift, qkv_weight, proj_weight, bias_table, pos_index,
    region_ids,
):
    frame_count, row_count, col_count, _ = frames_in.shape
    token_total = frame_count * row_count * col_count * lax.axis_size(ALL)
    both = (frames_in, grad_out)
    below, right, corner, x_tile, g_tile, pos_v, table_v, ids = edges(
        frames_in, grad_out, pos_index, bias_table.T, region_ids
    )
    below = shifted(below, -1, 0)
    right = shifted(right, 0, -1)
    corner = shifted(corner, -1, -1)
    ids = ids.reshape(2, 2, 8, 2, 8).transpose(1, 3, 0, 2, 4).reshape(N_WIN, WIN_TOK)
    bias, pos_t, *rest = gather_bias(
        pos_v, table_v, x_tile, g_tile, ids, norm_gain, norm_shift, qkv_weight, proj_weight
    )
    first_window, params = rest[:7], rest[7:]
    me = lax.axis_index("c").reshape(1)
    kept, sent, branch, back = main_call(
        x_tile, g_tile, below, right, corner, *params, bias, ids, pos_t, *first_window, me,
    )
    part = add_halves(kept, swap_cores(sent))
    plane = ("l", "h", "x")
    part = exchange(part.reshape(lax.axis_size(plane), -1, 128), plane)
    part, branch, back = lax.optimization_barrier((part, branch, back))
    part = exchange(sum_copies(part, lax.axis_size("z")), ("z",))
    flipped = [jnp.concatenate([a[1:], a[:1]], axis=0) for a in (branch, back)]
    above = shifted(jnp.stack([a[:, 12:, :12] for a in flipped]), 1, 0)
    left = shifted(jnp.stack([a[:, :12, 12:] for a in flipped]), 0, 1)
    angle = shifted(jnp.stack([a[:, 12:, 12:] for a in flipped]), 1, 1)
    part, above, left, angle = lax.optimization_barrier((part, above, left, angle))
    outs = []
    for n, a in enumerate(both):
        upper = jnp.concatenate([angle[n], above[n]], axis=2)
        lower = jnp.concatenate([left[n], flipped[n][:, :12, :12]], axis=2)
        moved = jnp.concatenate([upper, lower], axis=1)
        outs.append((a.astype(F32) + moved.astype(F32)).astype(BF16))

    own = exchange(sum_copies(part, lax.axis_size(plane)), plane).reshape(HALF, 128)
    own, outs = lax.optimization_barrier((own, outs))
    other = swap_cores(own)
    grad_qkv, grad_proj, table, gain, shift = unpack(me, own, other, token_total**-0.5)
    return outs[0], outs[1], grad_qkv, grad_proj, table.T, gain, shift


def solution(mesh):
    rows, cols = mesh.devices.shape
    fine = Mesh(mesh.devices.reshape(rows // 4, 2, 2, 2, cols // 2), ALL)
    tile = P(None, ROW, COL, None)
    return jax.shard_map(
        body,
        mesh=fine,
        in_specs=(tile, tile, P(), P(), P(), P(), P(), P(), P(None, ROW, COL)),
        out_specs=(tile, tile, P(), P(), P(), P(), P()),
        check_vma=False,
    )
```

```python
import functools

import jax
import jax.numpy as jnp
from jax import lax
from jax.experimental import pallas as pl
from jax.experimental.pallas import tpu as pltpu
from jax.sharding import Mesh
from jax.sharding import PartitionSpec as P

HEADS = 12
WIN_TOK = 128
TABLE_ROWS = 675
WIDTH = 384
HEAD_DIM = 32
GROUP = 128
N_WIN = 4
TOK = N_WIN * WIN_TOK
NORM_EPS = 1e-05
SCALE = HEAD_DIM**-0.5

ROW_PROJ = 9 * WIDTH
ROW_TABLE = 12 * WIDTH
ROW_NORM = ROW_TABLE + 96
PACK_ROWS = 4864
HALF = PACK_ROWS // 2

F32 = jnp.float32
BF16 = jnp.bfloat16
VMEM_LIMIT = 20 * 1024 * 1024

NN = (((1,), (0,)), ((), ()))
NT = (((1,), (1,)), ((), ()))
TN = (((0,), (0,)), ((), ()))


def mm(a, b, dims):
    return lax.dot_general(a, b, dims, preferred_element_type=F32)


def whole(n):
    return [pl.BlockSpec(memory_space=pltpu.VMEM)] * n


def in_vmem(shape, dtype):
    return pltpu.VMEM(shape, dtype)


def edge_kernel(
    x_ref, g_ref, pos_ref, table_ref, id_ref,
    below_ref, right_ref, corner_ref, x_s, g_s, pos_s, table_s, id_s, sems,
):
    pairs = (
        (x_ref, x_s), (g_ref, g_s), (pos_ref, pos_s), (table_ref, table_s), (id_ref, id_s),
    )
    copies = [pltpu.make_async_copy(a, b, sems.at[n]) for n, (a, b) in enumerate(pairs)]
    for copy in copies:
        copy.start()
    for n, ref in enumerate((x_s, g_s)):
        copies[n].wait()
        below_ref[n] = ref[:, 0:4, :, :].astype(F32)[:, :, 4:16, :].astype(BF16)
        right_ref[n] = ref[:, 4:16, 0:4, :]
        corner_ref[n] = ref[:, 0:4, 0:4, :]
    for copy in copies[2:]:
        copy.wait()


def edges(*args):
    return pl.pallas_call(
        edge_kernel,
        out_shape=(
            in_vmem((2, 2, 4, 12, WIDTH), BF16),
            in_vmem((2, 2, 12, 4, WIDTH), BF16),
            in_vmem((2, 2, 4, 4, WIDTH), BF16),
        )
        + tuple(in_vmem(a.shape, a.dtype) for a in args),
        in_specs=[pl.BlockSpec(memory_space=pltpu.HBM)] * 5,
        out_specs=tuple(whole(8)),
        scratch_shapes=[pltpu.SemaphoreType.DMA((5,))],
        compiler_params=pltpu.CompilerParams(vmem_limit_bytes=VMEM_LIMIT),
        cost_estimate=pl.CostEstimate(flops=0, bytes_accessed=1_200_000, transcendentals=0),
        name="edges",
    )(*(pltpu.with_memory_space_constraint(a, pltpu.HBM) for a in args))


def bias_kernel(
    pos_ref, table_ref, x_ref, g_ref, id_ref, gain_ref, shift_ref, wqkv_ref, wproj_ref,
    bias_ref, pos_t_ref, hat_ref, inv_ref, normed_ref, g0_ref, att_ref, gqkv_ref, sums_ref,
    gain_v, shift_v, wqkv_v, wproj_v, table_s, qkv_s, da_s, sems,
):
    pairs = ((wqkv_ref, wqkv_v), (wproj_ref, wproj_v), (gain_ref, gain_v), (shift_ref, shift_v))
    copies = [pltpu.make_async_copy(a, b, sems.at[n]) for n, (a, b) in enumerate(pairs)]
    for copy in copies:
        copy.start()
    pos_t_ref[...] = pos_ref[...].T
    table_s[...] = jnp.zeros_like(table_s)
    table_s[0:HEADS, 0:TABLE_ROWS] = table_ref[...]

    def rows(step, carry):
        at = pl.multiple_of(step * 8, 8)
        idx = pos_t_ref[pl.ds(at, 8), :]
        low = idx & 127
        high = idx >> 7
        for h in range(HEADS):
            got = None
            for k in range(6):
                chunk = jnp.broadcast_to(table_s[h : h + 1, k * 128 : (k + 1) * 128], (8, 128))
                part = jnp.take_along_axis(chunk, low, axis=1)
                got = part if k == 0 else jnp.where(high == k, part, got)
            bias_ref[h, pl.ds(at, 8), :] = got
        return carry

    lax.fori_loop(0, 16, rows, 0, unroll=2)
    for copy in copies:
        copy.wait()
    sums_ref[...] = jnp.zeros_like(sums_ref)
    first = slice(0, WIN_TOK)
    x = window_tokens(0, x_ref, None, None, None, 0, 0)
    g = window_tokens(1, g_ref, None, None, None, 0, 0)
    normalize(x, g, row_of(gain_v), row_of(shift_v), first, hat_ref, inv_ref, normed_ref, g0_ref)
    project(first, normed_ref, g0_ref, wqkv_v, wproj_v, qkv_s, da_s)
    shut = shut_pairs(id_ref, 0)
    for k in range(3):
        attend(k, first, shut, bias_ref, qkv_s, da_s, att_ref, gqkv_ref, sums_ref)


def gather_bias(pos_index, table_t, x, g, ids, *params):
    return pl.pallas_call(
        bias_kernel,
        out_shape=(
            in_vmem((HEADS, WIN_TOK, WIN_TOK), F32),
            in_vmem((WIN_TOK, WIN_TOK), jnp.int32),
            in_vmem((WIN_TOK, WIDTH), F32),
            in_vmem((WIN_TOK, 128), F32),
            in_vmem((WIN_TOK, WIDTH), BF16),
            in_vmem((WIN_TOK, WIDTH), BF16),
            in_vmem((3, WIN_TOK, GROUP), BF16),
            in_vmem((9, WIN_TOK, GROUP), BF16),
            in_vmem((16, WIN_TOK, WIN_TOK), F32),
        )
        + tuple(in_vmem(a.shape, a.dtype) for a in params),
        in_specs=whole(5) + [pl.BlockSpec(memory_space=pltpu.HBM)] * 4,
        out_specs=tuple(whole(13)),
        scratch_shapes=[
            pltpu.VMEM((16, 768), F32),
            pltpu.VMEM((9, WIN_TOK, GROUP), BF16),
            pltpu.VMEM((3, WIN_TOK, GROUP), BF16),
            pltpu.SemaphoreType.DMA((4,)),
        ],
        compiler_params=pltpu.CompilerParams(vmem_limit_bytes=VMEM_LIMIT),
        cost_estimate=pl.CostEstimate(flops=4_000_000, bytes_accessed=900_000, transcendentals=0),
        name="gather_bias",
    )(
        pos_index,
        table_t,
        x,
        g,
        ids,
        *(pltpu.with_memory_space_constraint(a, pltpu.HBM) for a in params),
    )


def row_of(ref):
    return jnp.concatenate([ref[k * 128 : (k + 1) * 128].reshape(1, 128) for k in range(3)], axis=1)


def window_tokens(n, tile_ref, below_ref, right_ref, corner_ref, wr, wc):
    def columns(rows, side):
        if wc == 0:
            return rows[:, :, 0:8, :]
        return jnp.concatenate([rows[:, :, 8:12, :], side().astype(F32)], axis=2)

    top = 4 + 8 * wr
    own = 8 - 4 * wr
    rows = columns(
        tile_ref[:, top : top + own, :, :].astype(F32)[:, :, 4:16, :],
        lambda: right_ref[n, :, top - 4 : top - 4 + own, :, :],
    )
    if wr == 1:
        lower = columns(below_ref[n].astype(F32), lambda: corner_ref[n])
        rows = jnp.concatenate([rows, lower], axis=1)
    return jnp.concatenate([rows[1:], rows[:1]], axis=0).reshape(WIN_TOK, WIDTH)


def store_tile(ref, tokens):
    for wr in range(2):
        pair = [
            tokens[(2 * wr + wc) * WIN_TOK : (2 * wr + wc + 1) * WIN_TOK].reshape(2, 8, 8, WIDTH)
            for wc in range(2)
        ]
        ref[:, 8 * wr : 8 * wr + 8, :, :] = jnp.concatenate(pair, axis=2).astype(BF16)


def normalize(x, g, gain, shift, rows, hat_s, inv_s, normed_s, g_s):
    centered = x - jnp.mean(x, axis=-1, keepdims=True)
    variance = jnp.mean(centered * centered, axis=-1, keepdims=True)
    inv_std = lax.rsqrt(variance + NORM_EPS)
    x_hat = centered * inv_std
    hat_s[rows, :] = x_hat
    inv_s[rows, :] = jnp.broadcast_to(inv_std, (WIN_TOK, 128))
    normed_s[rows, :] = (x_hat * gain + shift).astype(BF16)
    g_s[rows, :] = g.astype(BF16)


def shut_pairs(id_ref, w):
    ids = jnp.broadcast_to(id_ref[w : w + 1, :], (WIN_TOK, WIN_TOK))
    return jnp.where(ids.T == ids, 0.0, -1e30)


def project(rows, normed_s, g_s, wqkv_ref, wproj_ref, qkv_s, da_s):
    for p in range(3):
        part = mm(normed_s[rows, :], wqkv_ref[:, p * WIDTH : (p + 1) * WIDTH], NN).astype(BF16)
        for k in range(3):
            qkv_s[3 * p + k, rows, :] = part[:, k * GROUP : (k + 1) * GROUP]
    part = mm(g_s[rows, :], wproj_ref[...], NT).astype(BF16)
    for k in range(3):
        da_s[k, rows, :] = part[:, k * GROUP : (k + 1) * GROUP]


def attend(k, rows, shut, bias_ref, qkv_s, da_s, att_s, gqkv_s, table_s):
    lane = lax.broadcasted_iota(jnp.int32, (WIN_TOK, GROUP), 1) // HEAD_DIM
    q = qkv_s[k, rows, :]
    key = qkv_s[3 + k, rows, :]
    v = qkv_s[6 + k, rows, :]
    da = da_s[k, rows, :]
    zero = jnp.zeros_like(q)
    q_all, key_all, v_all, da_all = (
        jnp.concatenate([jnp.where(lane == h, a, zero) for h in range(4)], axis=0)
        for a in (q, key, v, da)
    )
    score_all = mm(key_all, q, NT)
    grad_all = mm(v_all, da, NT)
    probs, grads = [], []
    for h in range(4):
        score = score_all[128 * h : 128 * h + 128] * SCALE + bias_ref[4 * k + h] + shut
        top = jnp.max(score, axis=0, keepdims=True)
        e = jnp.exp(score - top)
        prob = e * (1.0 / jnp.sum(e, axis=0, keepdims=True))
        grad_prob = grad_all[128 * h : 128 * h + 128]
        inner = jnp.sum(prob * grad_prob, axis=0, keepdims=True)
        grad_score = prob * (grad_prob - inner)
        table_s[4 * k + h] += grad_score
        probs.append(prob.astype(BF16))
        grads.append((grad_score * SCALE).astype(BF16))
    prob_rows = jnp.concatenate(probs, axis=0)
    grad_rows = jnp.concatenate(grads, axis=0)
    att_s[k, rows, :] = mm(prob_rows, v_all, TN).astype(BF16)
    gqkv_s[k, rows, :] = mm(grad_rows, key_all, TN).astype(BF16)
    gqkv_s[3 + k, rows, :] = mm(jnp.concatenate(grads, axis=1), q_all, NN).astype(BF16)
    gqkv_s[6 + k, rows, :] = mm(jnp.concatenate(probs, axis=1), da_all, NN).astype(BF16)


def main_kernel(
    x_ref, g_ref, below_ref, right_ref, corner_ref, gain_ref, shift_ref, wqkv_ref, wproj_ref, bias_ref, id_ref,
    pos_ref, hat0_ref, inv0_ref, normed0_ref, g0_ref, att0_ref, gqkv0_ref, table0_ref,
    me_ref, kept_ref, sent_ref, branch_ref, back_ref,
    att_s, hat_s, inv_s, normed_s, g_s, qkv_s, da_s, gqkv_s, table_s, shut_s, pack_ref,
):
    gain = row_of(gain_ref)
    shift = row_of(shift_ref)
    edge_refs = (below_ref, right_ref, corner_ref)
    first = slice(0, WIN_TOK)
    hat_s[first, :] = hat0_ref[...]
    inv_s[first, :] = inv0_ref[...]
    normed_s[first, :] = normed0_ref[...]
    g_s[first, :] = g0_ref[...]
    att_s[:, first, :] = att0_ref[...]
    gqkv_s[:, first, :] = gqkv0_ref[...]
    table_s[...] = table0_ref[...]
    for w in range(1, N_WIN):
        x = window_tokens(0, x_ref, *edge_refs, w // 2, w % 2)
        g = window_tokens(1, g_ref, *edge_refs, w // 2, w % 2)
        rows = slice(w * WIN_TOK, (w + 1) * WIN_TOK)
        normalize(x, g, gain, shift, rows, hat_s, inv_s, normed_s, g_s)
        shut_s[w] = shut_pairs(id_ref, w)
    project(slice(WIN_TOK, TOK), normed_s, g_s, wqkv_ref, wproj_ref, qkv_s, da_s)

    def step_of(step, carry):
        w = (step + 3) // 3
        rows = pl.ds(pl.multiple_of(w * WIN_TOK, WIN_TOK), WIN_TOK)
        attend(step % 3, rows, shut_s[w], bias_ref, qkv_s, da_s, att_s, gqkv_s, table_s)
        return carry

    lax.fori_loop(0, 9, step_of, 0, unroll=9)

    attended = jnp.concatenate([att_s[k] for k in range(3)], axis=1)
    store_tile(branch_ref, mm(attended, wproj_ref[...], NN))
    grad_proj = mm(attended, g_s[...], TN)
    for k in range(3):
        at = ROW_PROJ + k * WIDTH
        pack_ref[at : at + WIDTH, :] = grad_proj[:, k * GROUP : (k + 1) * GROUP].astype(BF16)

    grad_normed = None
    for p in range(3):
        grad_part = jnp.concatenate([gqkv_s[3 * p + k] for k in range(3)], axis=1)
        grad_w = mm(normed_s[...], grad_part, TN)
        for k in range(3):
            at = (3 * p + k) * WIDTH
            pack_ref[at : at + WIDTH, :] = grad_w[:, k * GROUP : (k + 1) * GROUP].astype(BF16)
        term = mm(grad_part, wqkv_ref[:, p * WIDTH : (p + 1) * WIDTH], NT)
        grad_normed = term if p == 0 else grad_normed + term
    x_hat = hat_s[...]
    grad_gain = jnp.sum(grad_normed * x_hat, axis=0, keepdims=True)
    grad_shift = jnp.sum(grad_normed, axis=0, keepdims=True)
    scaled = grad_normed * gain
    store_tile(
        back_ref,
        inv_s[:, 0:1]
        * (
            scaled
            - jnp.mean(scaled, axis=-1, keepdims=True)
            - x_hat * jnp.mean(scaled * x_hat, axis=-1, keepdims=True)
        ),
    )

    low_bins = lax.broadcasted_iota(jnp.int32, (128, WIN_TOK), 0)

    def bins(step, acc):
        at = pl.multiple_of(step * 8, 8)
        index = pos_ref[pl.ds(at, 8), :]
        block = jnp.swapaxes(table_s[:, pl.ds(at, 8), :], 0, 1)
        for n in range(0, 8, 2):
            left, right = [], []
            for j in (n, n + 1):
                idx = index[j : j + 1]
                high = idx >> 7
                terms = block[j]
                left.append(
                    jnp.concatenate([jnp.where(high == a, terms, 0.0) for a in range(6)], axis=0)
                )
                right.append(jnp.where(low_bins == (idx & 127), 1.0, 0.0))
            acc = acc + mm(
                jnp.concatenate(left, axis=1).astype(BF16),
                jnp.concatenate(right, axis=1).astype(BF16),
                NT,
            )
        return acc

    table = lax.fori_loop(0, WIN_TOK // 8, bins, jnp.zeros((96, 128), F32), unroll=8)
    pack_ref[ROW_TABLE : ROW_TABLE + 96, :] = table.astype(BF16)
    norm_rows = [a[:, k * 128 : (k + 1) * 128] for a in (grad_gain, grad_shift) for k in range(3)]
    norm_rows.append(jnp.zeros((10, 128), F32))
    pack_ref[ROW_NORM : ROW_NORM + 16, :] = jnp.concatenate(norm_rows, axis=0).astype(BF16)
    pack_ref[ROW_NORM + 16 :, :] = jnp.zeros((PACK_ROWS - ROW_NORM - 16, 128), BF16)
    me = me_ref[0]
    kept_ref[...] = pack_ref[pl.ds(pl.multiple_of(me * HALF, HALF), HALF), :]
    sent_ref[...] = pack_ref[pl.ds(pl.multiple_of((1 - me) * HALF, HALF), HALF), :]


def main_call(*args):
    return pl.pallas_call(
        main_kernel,
        out_shape=(
            in_vmem((HALF, 128), BF16),
            in_vmem((HALF, 128), BF16),
            in_vmem((2, 16, 16, WIDTH), BF16),
            in_vmem((2, 16, 16, WIDTH), BF16),
        ),
        in_specs=whole(len(args) - 1) + [pl.BlockSpec(memory_space=pltpu.SMEM)],
        out_specs=tuple(whole(4)),
        scratch_shapes=[
            pltpu.VMEM((3, TOK, GROUP), BF16),
            pltpu.VMEM((TOK, WIDTH), F32),
            pltpu.VMEM((TOK, 128), F32),
            pltpu.VMEM((TOK, WIDTH), BF16),
            pltpu.VMEM((TOK, WIDTH), BF16),
            pltpu.VMEM((9, TOK, GROUP), BF16),
            pltpu.VMEM((3, TOK, GROUP), BF16),
            pltpu.VMEM((9, TOK, GROUP), BF16),
            pltpu.VMEM((16, WIN_TOK, WIN_TOK), F32),
            pltpu.VMEM((N_WIN, WIN_TOK, WIN_TOK), F32),
            pltpu.VMEM((PACK_ROWS, 128), BF16),
        ],
        compiler_params=pltpu.CompilerParams(vmem_limit_bytes=VMEM_LIMIT),
        cost_estimate=pl.CostEstimate(
            flops=4_000_000_000, bytes_accessed=6_000_000, transcendentals=800_000
        ),
        name="block_pass",
    )(*args)


def unpack_kernel(
    factor, me_ref, own_ref, other_ref, qkv_ref, proj_ref, table_ref, gain_ref, shift_ref, pack_ref
):
    me = me_ref[0]
    pack_ref[pl.ds(pl.multiple_of(me * HALF, HALF), HALF), :] = own_ref[...]
    pack_ref[pl.ds(pl.multiple_of((1 - me) * HALF, HALF), HALF), :] = other_ref[...]
    for k in range(12):
        block = pack_ref[k * WIDTH : (k + 1) * WIDTH, :].astype(F32) * factor
        if k < 9:
            qkv_ref[:, k * 128 : (k + 1) * 128] = block
        else:
            proj_ref[:, (k - 9) * 128 : (k - 8) * 128] = block
    table = pack_ref[ROW_TABLE : ROW_TABLE + 96, :].astype(F32) * factor
    wide = jnp.concatenate([table[16 * a : 16 * a + 16] for a in range(6)], axis=1)
    table_ref[...] = wide[0:HEADS, 0:TABLE_ROWS]
    norm = pack_ref[ROW_NORM : ROW_NORM + 16, :].astype(F32) * factor
    for n, ref in enumerate((gain_ref, shift_ref)):
        for k in range(3):
            ref[k * 128 : (k + 1) * 128] = norm[3 * n + k]


def unpack(me, own, other, factor):
    return pl.pallas_call(
        functools.partial(unpack_kernel, factor),
        out_shape=(
            jax.ShapeDtypeStruct((WIDTH, 3 * WIDTH), F32),
            jax.ShapeDtypeStruct((WIDTH, WIDTH), F32),
            jax.ShapeDtypeStruct((HEADS, TABLE_ROWS), F32),
            jax.ShapeDtypeStruct((WIDTH,), F32),
            jax.ShapeDtypeStruct((WIDTH,), F32),
        ),
        in_specs=[pl.BlockSpec(memory_space=pltpu.SMEM)] + whole(2),
        out_specs=tuple(whole(5)),
        scratch_shapes=[pltpu.VMEM((PACK_ROWS, 128), BF16)],
        compiler_params=pltpu.CompilerParams(vmem_limit_bytes=VMEM_LIMIT),
        cost_estimate=pl.CostEstimate(flops=600_000, bytes_accessed=3_600_000, transcendentals=0),
        name="unpack_sums",
    )(me, own, other)


def add_kernel(a_ref, b_ref, out_ref):
    out_ref[...] = (a_ref[...].astype(F32) + b_ref[...].astype(F32)).astype(BF16)


def add_halves(a, b):
    return pl.pallas_call(
        add_kernel,
        out_shape=in_vmem((HALF, 128), BF16),
        in_specs=whole(2),
        out_specs=pl.BlockSpec(memory_space=pltpu.VMEM),
        compiler_params=pltpu.CompilerParams(vmem_limit_bytes=VMEM_LIMIT),
        cost_estimate=pl.CostEstimate(flops=300_000, bytes_accessed=1_800_000, transcendentals=0),
        name="add_halves",
    )(a, b)


def copies_kernel(parts_ref, out_ref):
    total = parts_ref[0].astype(F32)
    for n in range(1, parts_ref.shape[0]):
        total += parts_ref[n].astype(F32)
    total = total.astype(BF16)
    for n in range(out_ref.shape[0]):
        out_ref[n] = total


def sum_copies(parts, count):
    return pl.pallas_call(
        copies_kernel,
        out_shape=in_vmem((count,) + parts.shape[1:], BF16),
        in_specs=whole(1),
        out_specs=pl.BlockSpec(memory_space=pltpu.VMEM),
        compiler_params=pltpu.CompilerParams(vmem_limit_bytes=VMEM_LIMIT),
        cost_estimate=pl.CostEstimate(flops=300_000, bytes_accessed=1_200_000, transcendentals=0),
        name="sum_copies",
    )(parts)


ROW = ("z", "l", "c")
COL = ("h", "x")
ALL = ROW + COL


def shifted(value, row_step, col_step):
    rows = lax.axis_size(ROW)
    cols = lax.axis_size(COL)
    pairs = [
        (r * cols + c, ((r + row_step) % rows) * cols + (c + col_step) % cols)
        for r in range(rows)
        for c in range(cols)
    ]
    return lax.ppermute(value, ALL, pairs)


def exchange(parts, axes):
    return lax.all_to_all(parts, axes, 0, 0)


def swap_cores(value):
    count = lax.axis_size(ALL)
    cols = lax.axis_size(COL)
    return lax.ppermute(value, ALL, [(i, i ^ cols) for i in range(count)])


def body(
    frames_in, grad_out, norm_gain, norm_shift, qkv_weight, proj_weight, bias_table, pos_index,
    region_ids,
):
    frame_count, row_count, col_count, _ = frames_in.shape
    token_total = frame_count * row_count * col_count * lax.axis_size(ALL)
    both = (frames_in, grad_out)
    below, right, corner, x_tile, g_tile, pos_v, table_v, ids = edges(
        frames_in, grad_out, pos_index, bias_table.T, region_ids
    )
    below = shifted(below, -1, 0)
    right = shifted(right, 0, -1)
    corner = shifted(corner, -1, -1)
    ids = ids.reshape(2, 2, 8, 2, 8).transpose(1, 3, 0, 2, 4).reshape(N_WIN, WIN_TOK)
    bias, pos_t, *rest = gather_bias(
        pos_v, table_v, x_tile, g_tile, ids, norm_gain, norm_shift, qkv_weight, proj_weight
    )
    first_window, params = rest[:7], rest[7:]
    me = lax.axis_index("c").reshape(1)
    kept, sent, branch, back = main_call(
        x_tile, g_tile, below, right, corner, *params, bias, ids, pos_t, *first_window, me,
    )
    part = add_halves(kept, swap_cores(sent))
    plane = ("l", "h", "x")
    part = exchange(part.reshape(lax.axis_size(plane), -1, 128), plane)
    part, branch, back = lax.optimization_barrier((part, branch, back))
    part = exchange(sum_copies(part, lax.axis_size("z")), ("z",))
    flipped = [jnp.concatenate([a[1:], a[:1]], axis=0) for a in (branch, back)]
    above = shifted(jnp.stack([a[:, 12:, :12] for a in flipped]), 1, 0)
    left = shifted(jnp.stack([a[:, :12, 12:] for a in flipped]), 0, 1)
    angle = shifted(jnp.stack([a[:, 12:, 12:] for a in flipped]), 1, 1)
    part, above, left, angle = lax.optimization_barrier((part, above, left, angle))
    outs = []
    for n, a in enumerate(both):
        upper = jnp.concatenate([angle[n], above[n]], axis=2)
        lower = jnp.concatenate([left[n], flipped[n][:, :12, :12]], axis=2)
        moved = jnp.concatenate([upper, lower], axis=1)
        outs.append((a.astype(F32) + moved.astype(F32)).astype(BF16))

    own = exchange(sum_copies(part, lax.axis_size(plane)), plane).reshape(HALF, 128)
    own, outs = lax.optimization_barrier((own, outs))
    other = swap_cores(own)
    grad_qkv, grad_proj, table, gain, shift = unpack(me, own, other, token_total**-0.5)
    return outs[0], outs[1], grad_qkv, grad_proj, table.T, gain, shift


def solution(mesh):
    rows, cols = mesh.devices.shape
    fine = Mesh(mesh.devices.reshape(rows // 4, 2, 2, 2, cols // 2), ALL)
    tile = P(None, ROW, COL, None)
    return jax.shard_map(
        body,
        mesh=fine,
        in_specs=(tile, tile, P(), P(), P(), P(), P(), P(), P(None, ROW, COL)),
        out_specs=(tile, tile, P(), P(), P(), P(), P()),
        check_vma=False,
    )
```

```python
import functools

import jax
import jax.numpy as jnp
from jax import lax
from jax.experimental import pallas as pl
from jax.experimental.pallas import tpu as pltpu
from jax.sharding import Mesh
from jax.sharding import PartitionSpec as P

HEADS = 12
WIN_TOK = 128
TABLE_ROWS = 675
WIDTH = 384
HEAD_DIM = 32
GROUP = 128
N_WIN = 4
TOK = N_WIN * WIN_TOK
NORM_EPS = 1e-05
SCALE = HEAD_DIM**-0.5

ROW_PROJ = 9 * WIDTH
ROW_TABLE = 12 * WIDTH
ROW_NORM = ROW_TABLE + 96
PACK_ROWS = 4864
HALF = PACK_ROWS // 2

F32 = jnp.float32
BF16 = jnp.bfloat16
VMEM_LIMIT = 20 * 1024 * 1024

NN = (((1,), (0,)), ((), ()))
NT = (((1,), (1,)), ((), ()))
TN = (((0,), (0,)), ((), ()))


def mm(a, b, dims):
    return lax.dot_general(a, b, dims, preferred_element_type=F32)


def whole(n):
    return [pl.BlockSpec(memory_space=pltpu.VMEM)] * n


def in_vmem(shape, dtype):
    return pltpu.VMEM(shape, dtype)


def edge_kernel(
    x_ref, g_ref, pos_ref, table_ref, id_ref,
    below_ref, right_ref, corner_ref, x_s, g_s, pos_s, table_s, id_s, sems,
):
    pairs = (
        (x_ref, x_s), (g_ref, g_s), (pos_ref, pos_s), (table_ref, table_s), (id_ref, id_s),
    )
    copies = [pltpu.make_async_copy(a, b, sems.at[n]) for n, (a, b) in enumerate(pairs)]
    for copy in copies:
        copy.start()
    for n, ref in enumerate((x_s, g_s)):
        copies[n].wait()
        below_ref[n] = ref[:, 0:4, :, :].astype(F32)[:, :, 4:16, :].astype(BF16)
        right_ref[n] = ref[:, 4:16, 0:4, :]
        corner_ref[n] = ref[:, 0:4, 0:4, :]
    for copy in copies[2:]:
        copy.wait()


def edges(*args):
    return pl.pallas_call(
        edge_kernel,
        out_shape=(
            in_vmem((2, 2, 4, 12, WIDTH), BF16),
            in_vmem((2, 2, 12, 4, WIDTH), BF16),
            in_vmem((2, 2, 4, 4, WIDTH), BF16),
        )
        + tuple(in_vmem(a.shape, a.dtype) for a in args),
        in_specs=[pl.BlockSpec(memory_space=pltpu.HBM)] * 5,
        out_specs=tuple(whole(8)),
        scratch_shapes=[pltpu.SemaphoreType.DMA((5,))],
        compiler_params=pltpu.CompilerParams(vmem_limit_bytes=VMEM_LIMIT),
        cost_estimate=pl.CostEstimate(flops=0, bytes_accessed=1_200_000, transcendentals=0),
        name="edges",
    )(*(pltpu.with_memory_space_constraint(a, pltpu.HBM) for a in args))


def bias_kernel(
    pos_ref, table_ref, x_ref, g_ref, id_ref, gain_ref, shift_ref, wqkv_ref, wproj_ref,
    bias_ref, pos_t_ref, hat_ref, inv_ref, normed_ref, g0_ref, att_ref, gqkv_ref, sums_ref,
    gain_v, shift_v, wqkv_v, wproj_v, table_s, qkv_s, da_s, sems,
):
    pairs = ((wqkv_ref, wqkv_v), (wproj_ref, wproj_v), (gain_ref, gain_v), (shift_ref, shift_v))
    copies = [pltpu.make_async_copy(a, b, sems.at[n]) for n, (a, b) in enumerate(pairs)]
    for copy in copies:
        copy.start()
    pos_t_ref[...] = pos_ref[...].T
    table_s[...] = jnp.zeros_like(table_s)
    table_s[0:HEADS, 0:TABLE_ROWS] = table_ref[...]

    def rows(step, carry):
        at = pl.multiple_of(step * 8, 8)
        idx = pos_t_ref[pl.ds(at, 8), :]
        low = idx & 127
        high = idx >> 7
        for h in range(HEADS):
            got = None
            for k in range(6):
                chunk = jnp.broadcast_to(table_s[h : h + 1, k * 128 : (k + 1) * 128], (8, 128))
                part = jnp.take_along_axis(chunk, low, axis=1)
                got = part if k == 0 else jnp.where(high == k, part, got)
            bias_ref[h, pl.ds(at, 8), :] = got
        return carry

    lax.fori_loop(0, 16, rows, 0, unroll=4)
    for copy in copies:
        copy.wait()
    sums_ref[...] = jnp.zeros_like(sums_ref)
    first = slice(0, WIN_TOK)
    x = window_tokens(0, x_ref, None, None, None, 0, 0)
    g = window_tokens(1, g_ref, None, None, None, 0, 0)
    normalize(x, g, row_of(gain_v), row_of(shift_v), first, hat_ref, inv_ref, normed_ref, g0_ref)
    project(first, normed_ref, g0_ref, wqkv_v, wproj_v, qkv_s, da_s)
    shut = shut_pairs(id_ref, 0)
    for k in range(3):
        attend(k, first, shut, bias_ref, qkv_s, da_s, att_ref, gqkv_ref, sums_ref)


def gather_bias(pos_index, table_t, x, g, ids, *params):
    return pl.pallas_call(
        bias_kernel,
        out_shape=(
            in_vmem((HEADS, WIN_TOK, WIN_TOK), F32),
            in_vmem((WIN_TOK, WIN_TOK), jnp.int32),
            in_vmem((WIN_TOK, WIDTH), F32),
            in_vmem((WIN_TOK, 128), F32),
            in_vmem((WIN_TOK, WIDTH), BF16),
            in_vmem((WIN_TOK, WIDTH), BF16),
            in_vmem((3, WIN_TOK, GROUP), BF16),
            in_vmem((9, WIN_TOK, GROUP), BF16),
            in_vmem((16, WIN_TOK, WIN_TOK), F32),
        )
        + tuple(in_vmem(a.shape, a.dtype) for a in params),
        in_specs=whole(5) + [pl.BlockSpec(memory_space=pltpu.HBM)] * 4,
        out_specs=tuple(whole(13)),
        scratch_shapes=[
            pltpu.VMEM((16, 768), F32),
            pltpu.VMEM((9, WIN_TOK, GROUP), BF16),
            pltpu.VMEM((3, WIN_TOK, GROUP), BF16),
            pltpu.SemaphoreType.DMA((4,)),
        ],
        compiler_params=pltpu.CompilerParams(vmem_limit_bytes=VMEM_LIMIT),
        cost_estimate=pl.CostEstimate(flops=4_000_000, bytes_accessed=900_000, transcendentals=0),
        name="gather_bias",
    )(
        pos_index,
        table_t,
        x,
        g,
        ids,
        *(pltpu.with_memory_space_constraint(a, pltpu.HBM) for a in params),
    )


def row_of(ref):
    return jnp.concatenate([ref[k * 128 : (k + 1) * 128].reshape(1, 128) for k in range(3)], axis=1)


def window_tokens(n, tile_ref, below_ref, right_ref, corner_ref, wr, wc):
    def columns(rows, side):
        if wc == 0:
            return rows[:, :, 0:8, :]
        return jnp.concatenate([rows[:, :, 8:12, :], side().astype(F32)], axis=2)

    top = 4 + 8 * wr
    own = 8 - 4 * wr
    rows = columns(
        tile_ref[:, top : top + own, :, :].astype(F32)[:, :, 4:16, :],
        lambda: right_ref[n, :, top - 4 : top - 4 + own, :, :],
    )
    if wr == 1:
        lower = columns(below_ref[n].astype(F32), lambda: corner_ref[n])
        rows = jnp.concatenate([rows, lower], axis=1)
    return jnp.concatenate([rows[1:], rows[:1]], axis=0).reshape(WIN_TOK, WIDTH)


def store_tile(ref, tokens):
    for wr in range(2):
        pair = [
            tokens[(2 * wr + wc) * WIN_TOK : (2 * wr + wc + 1) * WIN_TOK].reshape(2, 8, 8, WIDTH)
            for wc in range(2)
        ]
        ref[:, 8 * wr : 8 * wr + 8, :, :] = jnp.concatenate(pair, axis=2).astype(BF16)


def normalize(x, g, gain, shift, rows, hat_s, inv_s, normed_s, g_s):
    centered = x - jnp.mean(x, axis=-1, keepdims=True)
    variance = jnp.mean(centered * centered, axis=-1, keepdims=True)
    inv_std = lax.rsqrt(variance + NORM_EPS)
    x_hat = centered * inv_std
    hat_s[rows, :] = x_hat
    inv_s[rows, :] = jnp.broadcast_to(inv_std, (WIN_TOK, 128))
    normed_s[rows, :] = (x_hat * gain + shift).astype(BF16)
    g_s[rows, :] = g.astype(BF16)


def shut_pairs(id_ref, w):
    ids = jnp.broadcast_to(id_ref[w : w + 1, :], (WIN_TOK, WIN_TOK))
    return jnp.where(ids.T == ids, 0.0, -1e30)


def project(rows, normed_s, g_s, wqkv_ref, wproj_ref, qkv_s, da_s):
    for p in range(3):
        part = mm(normed_s[rows, :], wqkv_ref[:, p * WIDTH : (p + 1) * WIDTH], NN).astype(BF16)
        for k in range(3):
            qkv_s[3 * p + k, rows, :] = part[:, k * GROUP : (k + 1) * GROUP]
    part = mm(g_s[rows, :], wproj_ref[...], NT).astype(BF16)
    for k in range(3):
        da_s[k, rows, :] = part[:, k * GROUP : (k + 1) * GROUP]


def attend(k, rows, shut, bias_ref, qkv_s, da_s, att_s, gqkv_s, table_s):
    lane = lax.broadcasted_iota(jnp.int32, (WIN_TOK, GROUP), 1) // HEAD_DIM
    q = qkv_s[k, rows, :]
    key = qkv_s[3 + k, rows, :]
    v = qkv_s[6 + k, rows, :]
    da = da_s[k, rows, :]
    zero = jnp.zeros_like(q)
    q_all, key_all, v_all, da_all = (
        jnp.concatenate([jnp.where(lane == h, a, zero) for h in range(4)], axis=0)
        for a in (q, key, v, da)
    )
    score_all = mm(key_all, q, NT)
    grad_all = mm(v_all, da, NT)
    probs, grads = [], []
    for h in range(4):
        score = score_all[128 * h : 128 * h + 128] * SCALE + bias_ref[4 * k + h] + shut
        top = jnp.max(score, axis=0, keepdims=True)
        e = jnp.exp(score - top)
        prob = e * (1.0 / jnp.sum(e, axis=0, keepdims=True))
        grad_prob = grad_all[128 * h : 128 * h + 128]
        inner = jnp.sum(prob * grad_prob, axis=0, keepdims=True)
        grad_score = prob * (grad_prob - inner)
        table_s[4 * k + h] += grad_score
        probs.append(prob.astype(BF16))
        grads.append((grad_score * SCALE).astype(BF16))
    prob_rows = jnp.concatenate(probs, axis=0)
    grad_rows = jnp.concatenate(grads, axis=0)
    att_s[k, rows, :] = mm(prob_rows, v_all, TN).astype(BF16)
    gqkv_s[k, rows, :] = mm(grad_rows, key_all, TN).astype(BF16)
    gqkv_s[3 + k, rows, :] = mm(jnp.concatenate(grads, axis=1), q_all, NN).astype(BF16)
    gqkv_s[6 + k, rows, :] = mm(jnp.concatenate(probs, axis=1), da_all, NN).astype(BF16)


def main_kernel(
    x_ref, g_ref, below_ref, right_ref, corner_ref, gain_ref, shift_ref, wqkv_ref, wproj_ref, bias_ref, id_ref,
    pos_ref, hat0_ref, inv0_ref, normed0_ref, g0_ref, att0_ref, gqkv0_ref, table0_ref,
    me_ref, kept_ref, sent_ref, branch_ref, back_ref,
    att_s, hat_s, inv_s, normed_s, g_s, qkv_s, da_s, gqkv_s, table_s, shut_s, pack_ref,
):
    gain = row_of(gain_ref)
    shift = row_of(shift_ref)
    edge_refs = (below_ref, right_ref, corner_ref)
    first = slice(0, WIN_TOK)
    hat_s[first, :] = hat0_ref[...]
    inv_s[first, :] = inv0_ref[...]
    normed_s[first, :] = normed0_ref[...]
    g_s[first, :] = g0_ref[...]
    att_s[:, first, :] = att0_ref[...]
    gqkv_s[:, first, :] = gqkv0_ref[...]
    table_s[...] = table0_ref[...]
    for w in range(1, N_WIN):
        x = window_tokens(0, x_ref, *edge_refs, w // 2, w % 2)
        g = window_tokens(1, g_ref, *edge_refs, w // 2, w % 2)
        rows = slice(w * WIN_TOK, (w + 1) * WIN_TOK)
        normalize(x, g, gain, shift, rows, hat_s, inv_s, normed_s, g_s)
        shut_s[w] = shut_pairs(id_ref, w)
    project(slice(WIN_TOK, TOK), normed_s, g_s, wqkv_ref, wproj_ref, qkv_s, da_s)

    def step_of(step, carry):
        w = (step + 3) // 3
        rows = pl.ds(pl.multiple_of(w * WIN_TOK, WIN_TOK), WIN_TOK)
        attend(step % 3, rows, shut_s[w], bias_ref, qkv_s, da_s, att_s, gqkv_s, table_s)
        return carry

    lax.fori_loop(0, 9, step_of, 0, unroll=9)

    attended = jnp.concatenate([att_s[k] for k in range(3)], axis=1)
    store_tile(branch_ref, mm(attended, wproj_ref[...], NN))
    grad_proj = mm(attended, g_s[...], TN)
    for k in range(3):
        at = ROW_PROJ + k * WIDTH
        pack_ref[at : at + WIDTH, :] = grad_proj[:, k * GROUP : (k + 1) * GROUP].astype(BF16)

    grad_normed = None
    for p in range(3):
        grad_part = jnp.concatenate([gqkv_s[3 * p + k] for k in range(3)], axis=1)
        grad_w = mm(normed_s[...], grad_part, TN)
        for k in range(3):
            at = (3 * p + k) * WIDTH
            pack_ref[at : at + WIDTH, :] = grad_w[:, k * GROUP : (k + 1) * GROUP].astype(BF16)
        term = mm(grad_part, wqkv_ref[:, p * WIDTH : (p + 1) * WIDTH], NT)
        grad_normed = term if p == 0 else grad_normed + term
    x_hat = hat_s[...]
    grad_gain = jnp.sum(grad_normed * x_hat, axis=0, keepdims=True)
    grad_shift = jnp.sum(grad_normed, axis=0, keepdims=True)
    scaled = grad_normed * gain
    store_tile(
        back_ref,
        inv_s[:, 0:1]
        * (
            scaled
            - jnp.mean(scaled, axis=-1, keepdims=True)
            - x_hat * jnp.mean(scaled * x_hat, axis=-1, keepdims=True)
        ),
    )

    low_bins = lax.broadcasted_iota(jnp.int32, (128, WIN_TOK), 0)

    def bins(step, acc):
        at = pl.multiple_of(step * 8, 8)
        index = pos_ref[pl.ds(at, 8), :]
        block = jnp.swapaxes(table_s[:, pl.ds(at, 8), :], 0, 1)
        for n in range(0, 8, 2):
            left, right = [], []
            for j in (n, n + 1):
                idx = index[j : j + 1]
                high = idx >> 7
                terms = block[j]
                left.append(
                    jnp.concatenate([jnp.where(high == a, terms, 0.0) for a in range(6)], axis=0)
                )
                right.append(jnp.where(low_bins == (idx & 127), 1.0, 0.0))
            acc = acc + mm(
                jnp.concatenate(left, axis=1).astype(BF16),
                jnp.concatenate(right, axis=1).astype(BF16),
                NT,
            )
        return acc

    table = lax.fori_loop(0, WIN_TOK // 8, bins, jnp.zeros((96, 128), F32), unroll=16)
    pack_ref[ROW_TABLE : ROW_TABLE + 96, :] = table.astype(BF16)
    norm_rows = [a[:, k * 128 : (k + 1) * 128] for a in (grad_gain, grad_shift) for k in range(3)]
    norm_rows.append(jnp.zeros((10, 128), F32))
    pack_ref[ROW_NORM : ROW_NORM + 16, :] = jnp.concatenate(norm_rows, axis=0).astype(BF16)
    pack_ref[ROW_NORM + 16 :, :] = jnp.zeros((PACK_ROWS - ROW_NORM - 16, 128), BF16)
    me = me_ref[0]
    kept_ref[...] = pack_ref[pl.ds(pl.multiple_of(me * HALF, HALF), HALF), :]
    sent_ref[...] = pack_ref[pl.ds(pl.multiple_of((1 - me) * HALF, HALF), HALF), :]


def main_call(*args):
    return pl.pallas_call(
        main_kernel,
        out_shape=(
            in_vmem((HALF, 128), BF16),
            in_vmem((HALF, 128), BF16),
            in_vmem((2, 16, 16, WIDTH), BF16),
            in_vmem((2, 16, 16, WIDTH), BF16),
        ),
        in_specs=whole(len(args) - 1) + [pl.BlockSpec(memory_space=pltpu.SMEM)],
        out_specs=tuple(whole(4)),
        scratch_shapes=[
            pltpu.VMEM((3, TOK, GROUP), BF16),
            pltpu.VMEM((TOK, WIDTH), F32),
            pltpu.VMEM((TOK, 128), F32),
            pltpu.VMEM((TOK, WIDTH), BF16),
            pltpu.VMEM((TOK, WIDTH), BF16),
            pltpu.VMEM((9, TOK, GROUP), BF16),
            pltpu.VMEM((3, TOK, GROUP), BF16),
            pltpu.VMEM((9, TOK, GROUP), BF16),
            pltpu.VMEM((16, WIN_TOK, WIN_TOK), F32),
            pltpu.VMEM((N_WIN, WIN_TOK, WIN_TOK), F32),
            pltpu.VMEM((PACK_ROWS, 128), BF16),
        ],
        compiler_params=pltpu.CompilerParams(vmem_limit_bytes=VMEM_LIMIT),
        cost_estimate=pl.CostEstimate(
            flops=4_000_000_000, bytes_accessed=6_000_000, transcendentals=800_000
        ),
        name="block_pass",
    )(*args)


def unpack_kernel(
    factor, me_ref, own_ref, other_ref, qkv_ref, proj_ref, table_ref, gain_ref, shift_ref, pack_ref
):
    me = me_ref[0]
    pack_ref[pl.ds(pl.multiple_of(me * HALF, HALF), HALF), :] = own_ref[...]
    pack_ref[pl.ds(pl.multiple_of((1 - me) * HALF, HALF), HALF), :] = other_ref[...]
    for k in range(12):
        block = pack_ref[k * WIDTH : (k + 1) * WIDTH, :].astype(F32) * factor
        if k < 9:
            qkv_ref[:, k * 128 : (k + 1) * 128] = block
        else:
            proj_ref[:, (k - 9) * 128 : (k - 8) * 128] = block
    table = pack_ref[ROW_TABLE : ROW_TABLE + 96, :].astype(F32) * factor
    wide = jnp.concatenate([table[16 * a : 16 * a + 16] for a in range(6)], axis=1)
    table_ref[...] = wide[0:HEADS, 0:TABLE_ROWS]
    norm = pack_ref[ROW_NORM : ROW_NORM + 16, :].astype(F32) * factor
    for n, ref in enumerate((gain_ref, shift_ref)):
        for k in range(3):
            ref[k * 128 : (k + 1) * 128] = norm[3 * n + k]


def unpack(me, own, other, factor):
    return pl.pallas_call(
        functools.partial(unpack_kernel, factor),
        out_shape=(
            jax.ShapeDtypeStruct((WIDTH, 3 * WIDTH), F32),
            jax.ShapeDtypeStruct((WIDTH, WIDTH), F32),
            jax.ShapeDtypeStruct((HEADS, TABLE_ROWS), F32),
            jax.ShapeDtypeStruct((WIDTH,), F32),
            jax.ShapeDtypeStruct((WIDTH,), F32),
        ),
        in_specs=[pl.BlockSpec(memory_space=pltpu.SMEM)] + whole(2),
        out_specs=tuple(whole(5)),
        scratch_shapes=[pltpu.VMEM((PACK_ROWS, 128), BF16)],
        compiler_params=pltpu.CompilerParams(vmem_limit_bytes=VMEM_LIMIT),
        cost_estimate=pl.CostEstimate(flops=600_000, bytes_accessed=3_600_000, transcendentals=0),
        name="unpack_sums",
    )(me, own, other)


def add_kernel(a_ref, b_ref, out_ref):
    out_ref[...] = (a_ref[...].astype(F32) + b_ref[...].astype(F32)).astype(BF16)


def add_halves(a, b):
    return pl.pallas_call(
        add_kernel,
        out_shape=in_vmem((HALF, 128), BF16),
        in_specs=whole(2),
        out_specs=pl.BlockSpec(memory_space=pltpu.VMEM),
        compiler_params=pltpu.CompilerParams(vmem_limit_bytes=VMEM_LIMIT),
        cost_estimate=pl.CostEstimate(flops=300_000, bytes_accessed=1_800_000, transcendentals=0),
        name="add_halves",
    )(a, b)


def copies_kernel(parts_ref, out_ref):
    total = parts_ref[0].astype(F32)
    for n in range(1, parts_ref.shape[0]):
        total += parts_ref[n].astype(F32)
    total = total.astype(BF16)
    for n in range(out_ref.shape[0]):
        out_ref[n] = total


def sum_copies(parts, count):
    return pl.pallas_call(
        copies_kernel,
        out_shape=in_vmem((count,) + parts.shape[1:], BF16),
        in_specs=whole(1),
        out_specs=pl.BlockSpec(memory_space=pltpu.VMEM),
        compiler_params=pltpu.CompilerParams(vmem_limit_bytes=VMEM_LIMIT),
        cost_estimate=pl.CostEstimate(flops=300_000, bytes_accessed=1_200_000, transcendentals=0),
        name="sum_copies",
    )(parts)


ROW = ("z", "l", "c")
COL = ("h", "x")
ALL = ROW + COL


def shifted(value, row_step, col_step):
    rows = lax.axis_size(ROW)
    cols = lax.axis_size(COL)
    pairs = [
        (r * cols + c, ((r + row_step) % rows) * cols + (c + col_step) % cols)
        for r in range(rows)
        for c in range(cols)
    ]
    return lax.ppermute(value, ALL, pairs)


def exchange(parts, axes):
    return lax.all_to_all(parts, axes, 0, 0)


def swap_cores(value):
    count = lax.axis_size(ALL)
    cols = lax.axis_size(COL)
    return lax.ppermute(value, ALL, [(i, i ^ cols) for i in range(count)])


def body(
    frames_in, grad_out, norm_gain, norm_shift, qkv_weight, proj_weight, bias_table, pos_index,
    region_ids,
):
    frame_count, row_count, col_count, _ = frames_in.shape
    token_total = frame_count * row_count * col_count * lax.axis_size(ALL)
    both = (frames_in, grad_out)
    below, right, corner, x_tile, g_tile, pos_v, table_v, ids = edges(
        frames_in, grad_out, pos_index, bias_table.T, region_ids
    )
    below = shifted(below, -1, 0)
    right = shifted(right, 0, -1)
    corner = shifted(corner, -1, -1)
    ids = ids.reshape(2, 2, 8, 2, 8).transpose(1, 3, 0, 2, 4).reshape(N_WIN, WIN_TOK)
    bias, pos_t, *rest = gather_bias(
        pos_v, table_v, x_tile, g_tile, ids, norm_gain, norm_shift, qkv_weight, proj_weight
    )
    first_window, params = rest[:7], rest[7:]
    me = lax.axis_index("c").reshape(1)
    kept, sent, branch, back = main_call(
        x_tile, g_tile, below, right, corner, *params, bias, ids, pos_t, *first_window, me,
    )
    part = add_halves(kept, swap_cores(sent))
    plane = ("l", "h", "x")
    part = exchange(part.reshape(lax.axis_size(plane), -1, 128), plane)
    part, branch, back = lax.optimization_barrier((part, branch, back))
    part = exchange(sum_copies(part, lax.axis_size("z")), ("z",))
    flipped = [jnp.concatenate([a[1:], a[:1]], axis=0) for a in (branch, back)]
    above = shifted(jnp.stack([a[:, 12:, :12] for a in flipped]), 1, 0)
    left = shifted(jnp.stack([a[:, :12, 12:] for a in flipped]), 0, 1)
    angle = shifted(jnp.stack([a[:, 12:, 12:] for a in flipped]), 1, 1)
    part, above, left, angle = lax.optimization_barrier((part, above, left, angle))
    outs = []
    for n, a in enumerate(both):
        upper = jnp.concatenate([angle[n], above[n]], axis=2)
        lower = jnp.concatenate([left[n], flipped[n][:, :12, :12]], axis=2)
        moved = jnp.concatenate([upper, lower], axis=1)
        outs.append((a.astype(F32) + moved.astype(F32)).astype(BF16))

    own = exchange(sum_copies(part, lax.axis_size(plane)), plane).reshape(HALF, 128)
    own, outs = lax.optimization_barrier((own, outs))
    other = swap_cores(own)
    grad_qkv, grad_proj, table, gain, shift = unpack(me, own, other, token_total**-0.5)
    return outs[0], outs[1], grad_qkv, grad_proj, table.T, gain, shift


def solution(mesh):
    rows, cols = mesh.devices.shape
    fine = Mesh(mesh.devices.reshape(rows // 4, 2, 2, 2, cols // 2), ALL)
    tile = P(None, ROW, COL, None)
    return jax.shard_map(
        body,
        mesh=fine,
        in_specs=(tile, tile, P(), P(), P(), P(), P(), P(), P(None, ROW, COL)),
        out_specs=(tile, tile, P(), P(), P(), P(), P()),
        check_vma=False,
    )
```
